256 devices in a mesh: blk: 16 (over x, z_hi), uly: 16 (over z_lo, y, core).
Axes of the slice: x: 4, y: 4, z: 8 (z_hi: 4, z_lo: 2; z = z_hi * 2 + z_lo), core: 2. Of those that a mesh axis runs over, the one named last changes fastest.
Arguments:
- query_rows: bfloat16 [16384, 2048], P(('blk', 'uly')), may hold values from -30 to 30
- key_rows: bfloat16 [16384, 128], P(('blk', 'uly')), may hold values from -20 to 20
- value_rows: bfloat16 [16384, 128], P(('blk', 'uly')), may hold values from -6 to 6
- saved_out: bfloat16 [16384, 2048], P(('blk', 'uly')), may hold values from -6 to 6
- out_grad: bfloat16 [16384, 2048], P(('blk', 'uly')), may hold values from -6 to 6
- doc_lengths: int32 [64], replicated, may hold values from 1 to 512, 16384 in all
Outputs:
- query_grad: bfloat16 [16384, 2048], P(('blk', 'uly'))
- key_grad: bfloat16 [16384, 128], P(('blk', 'uly'))
- value_grad: bfloat16 [16384, 128], P(('blk', 'uly'))
The draws below stay inside these ranges and needn't reach their ends.
Inputs may be any that keep to these rules, and one draw needn't show every extreme that they name: `doc_lengths`: lengths of the documents in order of position; they sum to 16384 and the longest is exactly 512.
All inputs are finite; a program needn't handle non-finite values.
Results may differ from the reference program's by a relative error of at most 0.011.
Values may be sent and summed in bfloat16 or wider, within the bound.
No kernel may reach another device: no remote copies, remote signals or barrier semaphores. Data moves between devices by JAX's collectives and lax.ppermute only.
A program may use at most 64 MiB of HBM per device.

```python
import math
import jax
import jax.numpy as jnp
import numpy as np
from jax import lax

DH = 128
HQ = 16
KVH = 1
REACH = 1
LENGTH = 16384
MOST = 512
NDOCS = 64
N_BLK = 16


def draw_query_rows(key, part):
    key = jax.random.fold_in(key, 3)
    group_size = HQ // KVH
    base = jax.random.truncated_normal(key, -5.0, 5.0, (LENGTH, KVH, group_size, DH), jnp.float32)
    return base.reshape(LENGTH, HQ * DH).astype(jnp.bfloat16)


def draw_key_rows(key, part):
    key = jax.random.fold_in(key, 5)
    base = jax.random.truncated_normal(key, -5.0, 5.0, (LENGTH, KVH, 1, DH), jnp.float32)
    return base.reshape(LENGTH, KVH * DH).astype(jnp.bfloat16)


def block_levels(stream_key, shape, split, smallest, largest):
    loudness, own = 1.0, jax.random.fold_in(stream_key, 6)
    for dim, parts in split:
        heights = jnp.exp(jax.random.uniform(jax.random.fold_in(own, dim), (parts,), jnp.float32, smallest / len(split), largest / len(split)))
        loudness = loudness * jnp.repeat(heights, shape[dim] // parts).reshape([-1 if axis == dim else 1 for axis in range(len(shape))])
    return loudness


def split_up(number_of, total, most, slope):
    portions = [(1 << 20) // math.isqrt(rank ** slope) + 1 for rank in range(2, number_of + 1)]
    rest, counts = total - most - (number_of - 1), [1] * (number_of - 1)
    while rest > 0:
        movable = [i for i in range(number_of - 1) if counts[i] < most]
        pool, remaining = sum([portions[i] for i in movable]), rest
        for i in movable:
            extra = min(most - counts[i], max(1, remaining * portions[i] // pool), rest)
            counts[i] = counts[i] + extra
            rest = rest - extra
    return np.array([most] + counts)


def ragged_sizes(key, amount, total, reach, lean):
    if amount == 2:
        one = jax.random.randint(key, (), max(1, total - reach), min(reach, total - 1) + 1)
        return jnp.stack([one, total - one])
    tallies = jnp.asarray(split_up(amount, total, reach, lean), jnp.int32)
    couples = (amount - 1) // 2
    giver, taker = tallies[1:1 + 2 * couples:2], tallies[2:2 + 2 * couples:2]
    margin = jnp.minimum(giver - 1, reach - taker)
    moved = jax.random.randint(jax.random.fold_in(key, 1), (couples,), 0, 1 << 20) % (margin + 1)
    tallies = tallies.at[1:1 + 2 * couples:2].set(giver - moved).at[2:2 + 2 * couples:2].set(taker + moved)
    return tallies[jax.random.permutation(jax.random.fold_in(key, 2), amount)]


def gaussian(key, extent, deviation, most, split=(), held_as=jnp.bfloat16):
    drawn = jax.random.normal(key, extent, jnp.float32) * deviation
    if len(split) > 0:
        drawn = block_levels(key, extent, split, -0.22, 0.18) * drawn
    return jnp.clip(drawn, min=-most, max=most).astype(held_as)


def setup_inputs(seed: int = 0) -> dict:
    key_list = jax.random.split(jax.random.key(seed), 7)
    return {
        "query_rows": draw_query_rows(jax.random.fold_in(key_list[6], 71), 0),
        "key_rows": draw_key_rows(jax.random.fold_in(key_list[6], 71), 0),
        "value_rows": gaussian(key_list[2], (LENGTH, KVH * DH), 1.0, 6.0, ((0, 256),)),
        "saved_out": gaussian(key_list[3], (LENGTH, HQ * DH), 1.0, 6.0, ((0, 256),)),
        "out_grad": gaussian(key_list[4], (LENGTH, HQ * DH), 1.0, 6.0, ((0, 256),)),
        "doc_lengths": ragged_sizes(key_list[5], NDOCS, LENGTH, MOST, 2).astype(jnp.int32),
    }


MASKED_SCORE = -1e+30

def rounded(values):
    return lax.optimization_barrier(values.astype(jnp.bfloat16)).astype(jnp.float32)

def reference(query_rows, key_rows, value_rows, saved_out, out_grad, doc_lengths):
    half_rows = LENGTH // (2 * N_BLK)
    block_rows = 2 * half_rows
    group_size = HQ // KVH
    scaling = 1.0 / math.sqrt(DH)
    places = jnp.arange(LENGTH, dtype=jnp.int32)
    owners = places // block_rows
    offsets = places % block_rows
    pos_of_row = jnp.where(offsets < half_rows, owners * half_rows + offsets, (2 * N_BLK - 1 - owners) * half_rows + offsets - half_rows).astype(jnp.int32)
    blocks = places // half_rows
    offset = places % half_rows
    row_of_pos = jnp.where(blocks < N_BLK, blocks * block_rows + offset, (2 * N_BLK - 1 - blocks) * block_rows + half_rows + offset).astype(jnp.int32)
    doc_ends = jnp.cumsum(doc_lengths)
    doc_ids = lax.optimization_barrier(jnp.sum((places[:, None] >= doc_ends[None, :]).astype(jnp.int32), axis=1))
    query_all = query_rows[row_of_pos].reshape(LENGTH, KVH, group_size, DH)
    key_all = key_rows[row_of_pos].reshape(LENGTH, KVH, DH)
    value_all = value_rows[row_of_pos].reshape(LENGTH, KVH, DH)
    saved_all = saved_out[row_of_pos].reshape(LENGTH, KVH, group_size, DH)
    grad_all = out_grad[row_of_pos].reshape(LENGTH, KVH, group_size, DH)
    row_dot = lax.optimization_barrier(jnp.sum(grad_all.astype(jnp.float32) * saved_all.astype(jnp.float32), axis=-1))
    query_parts = []
    key_total = jnp.zeros((LENGTH, KVH, DH), jnp.float32)
    value_total = jnp.zeros((LENGTH, KVH, DH), jnp.float32)
    for block_index in range(2 * N_BLK):
        row_start = block_index * half_rows
        row_stop = row_start + half_rows
        key_start = max(0, block_index - REACH) * half_rows
        visible = (doc_ids[row_start:row_stop, None] == doc_ids[None, key_start:row_stop]) & (places[row_start:row_stop, None] >= places[None, key_start:row_stop])
        query_block = query_all[row_start:row_stop].astype(jnp.float32)
        grad_block = grad_all[row_start:row_stop].astype(jnp.float32)
        key_block = key_all[key_start:row_stop].astype(jnp.float32)
        value_block = value_all[key_start:row_stop].astype(jnp.float32)
        scores = jnp.einsum('qgjd,kgd->gjqk', query_block, key_block) * scaling
        row_max = lax.optimization_barrier(jnp.max(jnp.where(visible, scores, MASKED_SCORE), axis=-1))
        row_sum = lax.optimization_barrier(jnp.sum(jnp.where(visible, jnp.exp(scores - row_max[..., None]), 0.0), axis=-1))
        log_norm = row_max + jnp.log(row_sum)
        weights = jnp.where(visible, jnp.exp(scores - log_norm[..., None]), 0.0)
        grad_scores = jnp.einsum('qgjd,kgd->gjqk', grad_block, value_block)
        dot_block = jnp.transpose(row_dot[row_start:row_stop], (1, 2, 0))
        score_grads = rounded(weights * (grad_scores - dot_block[..., None]))
        weights = rounded(weights)
        value_total = value_total.at[key_start:row_stop].add(jnp.einsum('gjqk,qgjd->kgd', weights, grad_block))
        key_total = key_total.at[key_start:row_stop].add(jnp.einsum('gjqk,qgjd->kgd', score_grads, query_block) * scaling)
        query_parts.append(jnp.einsum('gjqk,kgd->qgjd', score_grads, key_block) * scaling)
    query_pos = jnp.concatenate(query_parts, axis=0).reshape(LENGTH, HQ * DH)
    query_grad = query_pos[pos_of_row].astype(jnp.bfloat16)
    key_grad = key_total.reshape(LENGTH, KVH * DH)[pos_of_row].astype(jnp.bfloat16)
    value_grad = value_total.reshape(LENGTH, KVH * DH)[pos_of_row].astype(jnp.bfloat16)
    return (query_grad, key_grad, value_grad)
```

```python
import math

import jax
import jax.numpy as jnp
from jax import lax
from jax.experimental import pallas as pl
from jax.experimental.pallas import tpu as pltpu
from jax.sharding import PartitionSpec as P

DH = 128
HQ = 16
ROWS = 64
CHUNKS = 256
CHIPS = CHUNKS // 2
HALF_CHUNKS = 8
HALVES = CHUNKS // HALF_CHUNKS
COLS = HQ * ROWS
CHIP_ROWS = 2 * ROWS
WINDOW = 5 * CHIP_ROWS
PAST = 4 * CHIP_ROWS
TILE = 256
NEG = -1e30
SCALING = 1.0 / math.sqrt(DH)
EXP2_SCALING = SCALING * math.log2(math.e)
AXES = ("blk", "uly")
STEPS = ((1, 4), (2, 3))


def device_of(chunk):
    half, place = divmod(chunk, HALF_CHUNKS)
    if half < HALVES // 2:
        return half * 16 + place
    return (HALVES - 1 - half) * 16 + 8 + place


def swap_cores(x):
    return lax.ppermute(x, "uly", [(i, i ^ 1) for i in range(16)])


def move_chips(x, steps, sign):
    pairs = []
    for chunk in range(CHUNKS):
        chip, core = divmod(chunk, 2)
        target = chip + sign * steps[core]
        if 0 <= target < CHIPS:
            pairs.append((device_of(chunk), device_of(2 * target + core)))
    return lax.ppermute(x, AXES, pairs)


def dot_nt(a, b):
    return lax.dot_general(a, b, (((1,), (1,)), ((), ())), preferred_element_type=jnp.float32)


def dot_nn(a, b):
    return lax.dot_general(a, b, (((1,), (0,)), ((), ())), preferred_element_type=jnp.float32)


def dot_tn(a, b):
    return lax.dot_general(a, b, (((0,), (0,)), ((), ())), preferred_element_type=jnp.float32)


def prepare_kernel(q_ref, o_ref, g_ref, len_ref, q2_ref, g2_ref, dot_ref, bias_ref):
    blk = lax.axis_index("blk")
    uly = lax.axis_index("uly")
    core = lax.rem(uly, 2)
    place = lax.rem(uly, HALF_CHUNKS)
    half = jnp.where(uly < HALF_CHUNKS, blk, HALVES - 1 - blk)
    chunk = half * HALF_CHUNKS + place
    chip = chunk // 2

    ones = jnp.ones((8, DH), jnp.bfloat16)
    for h in range(HQ):
        cols = slice(h * DH, (h + 1) * DH)
        rows = slice(h * ROWS, (h + 1) * ROWS)
        grad = g_ref[:, cols]
        q2_ref[rows, :] = q_ref[:, cols]
        g2_ref[rows, :] = grad
        prod = grad.astype(jnp.float32) * o_ref[:, cols].astype(jnp.float32)
        high = prod.astype(jnp.bfloat16)
        low = (prod - high.astype(jnp.float32)).astype(jnp.bfloat16)
        dot_ref[:, rows] = dot_nt(ones, high) + dot_nt(ones, low)

    lens = jnp.broadcast_to(len_ref[...].astype(jnp.float32), (64, 64))
    doc = lax.broadcasted_iota(jnp.int32, (64, 64), 0)
    other = lax.broadcasted_iota(jnp.int32, (64, 64), 1)
    starts = jnp.sum(jnp.where(other < doc, lens, 0.0), axis=1, keepdims=True).astype(jnp.int32)
    lane = lax.broadcasted_iota(jnp.int32, (1, DH), 1)
    here = chunk * ROWS + lax.rem(lane, ROWS)
    first = jnp.max(jnp.where(starts <= here, starts, 0), axis=0, keepdims=True)
    index = lax.broadcasted_iota(jnp.int32, (ROWS, DH), 0)
    for part in range(WINDOW // ROWS):
        group, side = divmod(part, 2)
        if group == 4:
            back, owner = 0, core
        elif group < 2:
            back, owner = jnp.where(core == 0, STEPS[group][0], STEPS[group][1]), core
        else:
            back, owner = jnp.where(core == 0, STEPS[group - 2][1], STEPS[group - 2][0]), 1 - core
        held = owner if side == 0 else 1 - owner
        where = (2 * (chip - back) + held) * ROWS + index
        seen = (where >= first) & (where <= here)
        bias_ref[part * ROWS : (part + 1) * ROWS, :] = jnp.where(seen, 0.0, NEG)


def main_kernel(q2_ref, g2_ref, dot_ref, bias_ref, z_ref, y_ref, w_ref,
                keep_ref, give_ref, p_ref, ds_ref, s_ref):
    def keys(part, cols):
        ref, at = ((z_ref, 0), (z_ref, 1), (y_ref, 0), (y_ref, 1), (w_ref, 0))[part]
        return ref[at * CHIP_ROWS : (at + 1) * CHIP_ROWS, cols]

    parts = range(WINDOW // CHIP_ROWS)
    key_cols, value_cols = slice(0, DH), slice(DH, 2 * DH)

    def folded(x, op):
        return op(x.reshape(CHIP_ROWS // 8, 8, TILE), axis=0)

    for tile in range(COLS // TILE):
        cols = slice(tile * TILE, (tile + 1) * TILE)
        query = q2_ref[cols, :]
        grad = g2_ref[cols, :]
        top = None
        for part in parts:
            bias = bias_ref[part * CHIP_ROWS : (part + 1) * CHIP_ROWS, :]
            scores = dot_nt(keys(part, key_cols), query) + jnp.concatenate([bias, bias], axis=1)
            s_ref[tile, part] = scores
            part_top = folded(scores, jnp.max)
            top = part_top if top is None else jnp.maximum(top, part_top)
        top = jnp.max(top, axis=0, keepdims=True)
        total = None
        for part in parts:
            weights = jnp.exp2((s_ref[tile, part] - top) * EXP2_SCALING)
            s_ref[tile, part] = weights
            part_total = folded(weights, jnp.sum)
            total = part_total if total is None else total + part_total
        inverse = 1.0 / jnp.sum(total, axis=0, keepdims=True)
        row_dot = dot_ref[0:1, cols]
        for part in parts:
            rows = slice(part * CHIP_ROWS, (part + 1) * CHIP_ROWS)
            weights = s_ref[tile, part] * inverse
            grads = weights * (dot_nt(keys(part, value_cols), grad) - row_dot)
            p_ref[rows, cols] = weights.astype(jnp.bfloat16)
            ds_ref[rows, cols] = grads.astype(jnp.bfloat16)
    for ref, at in ((keep_ref, 0), (give_ref, PAST // 2)):
        rows = slice(at, at + PAST // 2)
        ref[:, key_cols] = (dot_nn(ds_ref[rows, :], q2_ref[...]) * SCALING).astype(ref.dtype)
        ref[:, value_cols] = dot_nn(p_ref[rows, :], g2_ref[...]).astype(ref.dtype)


def finish_kernel(q2_ref, g2_ref, p_ref, ds_ref, z_ref, y_ref, w_ref, dq_ref, own_ref):
    key_cols, value_cols = slice(0, DH), slice(DH, 2 * DH)
    own = slice(PAST, WINDOW)
    own_ref[:, key_cols] = dot_nn(ds_ref[own, :], q2_ref[...]) * SCALING
    own_ref[:, value_cols] = dot_nn(p_ref[own, :], g2_ref[...])
    keys = jnp.concatenate([z_ref[:, key_cols], y_ref[:, key_cols], w_ref[:, key_cols]], axis=0)
    for tile in range(COLS // TILE):
        cols = slice(tile * TILE, (tile + 1) * TILE)
        grads = dot_tn(keys, ds_ref[:, cols]) * SCALING
        for j in range(TILE // DH):
            pair = grads[:, j * DH : (j + 1) * DH].T.astype(jnp.bfloat16)
            head = tile * (TILE // ROWS) + 2 * j
            dq_ref[:, head * DH : (head + 1) * DH] = pair[:ROWS]
            dq_ref[:, (head + 1) * DH : (head + 2) * DH] = pair[ROWS:]


def call(kernel, outs, scratch=(), flops=0, moved=0):
    vmem = pl.BlockSpec(memory_space=pltpu.VMEM)
    return lambda *args: pl.pallas_call(
        kernel,
        out_shape=outs,
        in_specs=[vmem] * len(args),
        out_specs=[vmem] * len(outs),
        scratch_shapes=list(scratch),
        compiler_params=pltpu.CompilerParams(vmem_limit_bytes=24 * 1024 * 1024),
        cost_estimate=pl.CostEstimate(flops=flops, bytes_accessed=moved, transcendentals=0),
    )(*args)


def on_device(query_rows, key_rows, value_rows, saved_out, out_grad, doc_lengths):
    shape = jax.ShapeDtypeStruct
    bf16, f32 = jnp.bfloat16, jnp.float32
    mine = jnp.concatenate([key_rows, value_rows], axis=1)
    own = jnp.concatenate([mine, swap_cores(mine)], axis=0)
    fetched = [move_chips(own, steps, 1) for steps in STEPS]
    q2, g2, row_dot, bias = call(
        prepare_kernel,
        [shape((COLS, DH), bf16), shape((COLS, DH), bf16), shape((8, COLS), f32), shape((WINDOW, DH), f32)],
        flops=10**9, moved=2 * 10**6,
    )(query_rows, saved_out, out_grad, doc_lengths.reshape(1, 64))
    near = jnp.concatenate(fetched, axis=0)
    far = swap_cores(near)
    keep, give, weights, grads = call(
        main_kernel,
        [shape((PAST // 2, 2 * DH), f32), shape((PAST // 2, 2 * DH), bf16),
         shape((WINDOW, COLS), bf16), shape((WINDOW, COLS), bf16)],
        [pltpu.VMEM((COLS // TILE, WINDOW // CHIP_ROWS, CHIP_ROWS, TILE), f32)],
        flops=10**9, moved=2 * 10**6,
    )(q2, g2, row_dot, bias, near, far, own)
    sums = (keep + swap_cores(give).astype(f32)).astype(bf16)
    back = [
        move_chips(sums[i * CHIP_ROWS : (i + 1) * CHIP_ROWS], steps, -1)
        for i, steps in enumerate(STEPS)
    ]
    query_grad, own_sums = call(
        finish_kernel,
        [shape((ROWS, HQ * DH), bf16), shape((CHIP_ROWS, 2 * DH), f32)],
        flops=10**9, moved=2 * 10**6,
    )(q2, g2, weights, grads, near, far, own)
    totals = own_sums + back[0].astype(f32) + back[1].astype(f32)
    result = totals[:ROWS] + swap_cores(totals[ROWS:].astype(bf16)).astype(f32)
    result = result.astype(bf16)
    return (query_grad, result[:, :DH], result[:, DH:])


def solution(mesh):
    placed = P(AXES, None)
    return jax.shard_map(
        on_device,
        mesh=mesh,
        in_specs=(placed,) * 5 + (P(),),
        out_specs=(placed,) * 3,
        check_vma=False,
    )
```

```python
import math

import jax
import jax.numpy as jnp
from jax import lax
from jax.experimental import pallas as pl
from jax.experimental.pallas import tpu as pltpu
from jax.sharding import PartitionSpec as P

DH = 128
HQ = 16
ROWS = 64
CHUNKS = 256
CHIPS = CHUNKS // 2
HALF_CHUNKS = 8
HALVES = CHUNKS // HALF_CHUNKS
COLS = HQ * ROWS
CHIP_ROWS = 2 * ROWS
WINDOW = 5 * CHIP_ROWS
PAST = 4 * CHIP_ROWS
TILE = 256
NEG = -1e30
SCALING = 1.0 / math.sqrt(DH)
EXP2_SCALING = SCALING * math.log2(math.e)
AXES = ("blk", "uly")
STEPS = ((2, 3), (1, 4))


def device_of(chunk):
    half, place = divmod(chunk, HALF_CHUNKS)
    if half < HALVES // 2:
        return half * 16 + place
    return (HALVES - 1 - half) * 16 + 8 + place


def swap_cores(x):
    return lax.ppermute(x, "uly", [(i, i ^ 1) for i in range(16)])


def move_chips(x, steps, sign):
    pairs = []
    for chunk in range(CHUNKS):
        chip, core = divmod(chunk, 2)
        target = (chip + sign * steps[core]) % CHIPS
        pairs.append((device_of(chunk), device_of(2 * target + core)))
    return lax.ppermute(x, AXES, pairs)


def dot_nt(a, b):
    return lax.dot_general(a, b, (((1,), (1,)), ((), ())), preferred_element_type=jnp.float32)


def dot_nn(a, b):
    return lax.dot_general(a, b, (((1,), (0,)), ((), ())), preferred_element_type=jnp.float32)


def dot_tn(a, b):
    return lax.dot_general(a, b, (((0,), (0,)), ((), ())), preferred_element_type=jnp.float32)


def pack_kernel(mine_ref, other_k_ref, other_v_ref, w_ref):
    w_ref[:ROWS, :] = mine_ref[...]
    w_ref[ROWS:, :DH] = other_k_ref[...]
    w_ref[ROWS:, DH:] = other_v_ref[...]


def prepare_kernel(q_hbm, o_hbm, g_hbm, len_hbm, q2_ref, g2_ref, dot_ref, bias_ref,
                   q_ref, o_ref, g_ref, len_ref, sems):
    pairs = ((len_hbm, len_ref), (g_hbm, g_ref), (o_hbm, o_ref), (q_hbm, q_ref))
    copies = [pltpu.make_async_copy(src, dst, sems.at[i]) for i, (src, dst) in enumerate(pairs)]
    for copy in copies:
        copy.start()
    blk = lax.axis_index("blk")
    uly = lax.axis_index("uly")
    core = lax.rem(uly, 2)
    place = lax.rem(uly, HALF_CHUNKS)
    half = jnp.where(uly < HALF_CHUNKS, blk, HALVES - 1 - blk)
    chunk = half * HALF_CHUNKS + place
    chip = chunk // 2

    copies[0].wait()
    lens = jnp.broadcast_to(len_ref[...].astype(jnp.float32), (64, 64))
    doc = lax.broadcasted_iota(jnp.int32, (64, 64), 0)
    other = lax.broadcasted_iota(jnp.int32, (64, 64), 1)
    starts = jnp.sum(jnp.where(other < doc, lens, 0.0), axis=1, keepdims=True).astype(jnp.int32)
    lane = lax.broadcasted_iota(jnp.int32, (1, DH), 1)
    here = chunk * ROWS + lax.rem(lane, ROWS)
    first = jnp.max(jnp.where(starts <= here, starts, 0), axis=0, keepdims=True)
    index = lax.broadcasted_iota(jnp.int32, (ROWS, DH), 0)
    for part in range(WINDOW // ROWS):
        group, side = divmod(part, 2)
        if group == 4:
            back, owner = 0, core
        elif group < 2:
            back, owner = jnp.where(core == 0, STEPS[group][0], STEPS[group][1]), core
        else:
            back, owner = jnp.where(core == 0, STEPS[group - 2][1], STEPS[group - 2][0]), 1 - core
        held = owner if side == 0 else 1 - owner
        where = (2 * (chip - back) + held) * ROWS + index
        seen = (where >= first) & (where <= here)
        bias_ref[part * ROWS : (part + 1) * ROWS, :] = jnp.where(seen, 0.0, NEG)

    for copy in copies[1:]:
        copy.wait()
    ones = jnp.ones((8, DH), jnp.bfloat16)
    for h in range(HQ):
        cols = slice(h * DH, (h + 1) * DH)
        rows = slice(h * ROWS, (h + 1) * ROWS)
        grad = g_ref[:, cols]
        q2_ref[rows, :] = q_ref[:, cols]
        g2_ref[rows, :] = grad
        prod = grad.astype(jnp.float32) * o_ref[:, cols].astype(jnp.float32)
        high = prod.astype(jnp.bfloat16)
        low = (prod - high.astype(jnp.float32)).astype(jnp.bfloat16)
        dot_ref[:, rows] = dot_nt(ones, high) + dot_nt(ones, low)


def main_kernel(q2_ref, g2_ref, dot_ref, bias_ref, z_ref, y_ref, w_ref,
                keep_ref, give_ref, p_ref, ds_ref, s_ref):
    def keys(part, cols):
        ref, at = ((z_ref, 0), (z_ref, 1), (y_ref, 0), (y_ref, 1), (w_ref, 0))[part]
        return ref[at * CHIP_ROWS : (at + 1) * CHIP_ROWS, cols]

    parts = range(WINDOW // CHIP_ROWS)
    key_cols, value_cols = slice(0, DH), slice(DH, 2 * DH)

    def folded(x, op):
        return op(x.reshape(CHIP_ROWS // 8, 8, TILE), axis=0)

    for tile in range(COLS // TILE):
        cols = slice(tile * TILE, (tile + 1) * TILE)
        query = q2_ref[cols, :]
        grad = g2_ref[cols, :]
        top = None
        for part in parts:
            bias = bias_ref[part * CHIP_ROWS : (part + 1) * CHIP_ROWS, :]
            scores = dot_nt(keys(part, key_cols), query) + jnp.concatenate([bias, bias], axis=1)
            s_ref[tile, part] = scores
            part_top = folded(scores, jnp.max)
            top = part_top if top is None else jnp.maximum(top, part_top)
        top = jnp.max(top, axis=0, keepdims=True)
        total = None
        for part in parts:
            weights = jnp.exp2((s_ref[tile, part] - top) * EXP2_SCALING)
            s_ref[tile, part] = weights
            part_total = folded(weights, jnp.sum)
            total = part_total if total is None else total + part_total
        inverse = 1.0 / jnp.sum(total, axis=0, keepdims=True)
        row_dot = dot_ref[0:1, cols]
        for part in parts:
            rows = slice(part * CHIP_ROWS, (part + 1) * CHIP_ROWS)
            weights = s_ref[tile, part] * inverse
            grads = weights * (dot_nt(keys(part, value_cols), grad) - row_dot)
            p_ref[rows, cols] = weights.astype(jnp.bfloat16)
            ds_ref[rows, cols] = grads.astype(jnp.bfloat16)
    for ref, at in ((keep_ref, 0), (give_ref, PAST // 2)):
        rows = slice(at, at + PAST // 2)
        ref[:, key_cols] = (dot_nn(ds_ref[rows, :], q2_ref[...]) * SCALING).astype(ref.dtype)
        ref[:, value_cols] = dot_nn(p_ref[rows, :], g2_ref[...]).astype(ref.dtype)


def finish_kernel(q2_ref, g2_ref, p_ref, ds_ref, z_ref, y_ref, w_ref, dq_ref, own_ref):
    key_cols, value_cols = slice(0, DH), slice(DH, 2 * DH)
    own = slice(PAST, WINDOW)
    own_ref[:, key_cols] = dot_nn(ds_ref[own, :], q2_ref[...]) * SCALING
    own_ref[:, value_cols] = dot_nn(p_ref[own, :], g2_ref[...])
    keys = jnp.concatenate([z_ref[:, key_cols], y_ref[:, key_cols], w_ref[:, key_cols]], axis=0)
    for tile in range(COLS // TILE):
        cols = slice(tile * TILE, (tile + 1) * TILE)
        grads = dot_tn(keys, ds_ref[:, cols]) * SCALING
        for j in range(TILE // DH):
            pair = grads[:, j * DH : (j + 1) * DH].T.astype(jnp.bfloat16)
            head = tile * (TILE // ROWS) + 2 * j
            dq_ref[:, head * DH : (head + 1) * DH] = pair[:ROWS]
            dq_ref[:, (head + 1) * DH : (head + 2) * DH] = pair[ROWS:]


def call(kernel, outs, scratch=(), space=pltpu.VMEM):
    vmem = pl.BlockSpec(memory_space=pltpu.VMEM)
    return lambda *args: pl.pallas_call(
        kernel,
        out_shape=outs,
        in_specs=[pl.BlockSpec(memory_space=space)] * len(args),
        out_specs=[vmem] * len(outs),
        scratch_shapes=list(scratch),
        compiler_params=pltpu.CompilerParams(vmem_limit_bytes=24 * 1024 * 1024),
        cost_estimate=pl.CostEstimate(flops=10**9, bytes_accessed=2 * 10**6, transcendentals=0),
    )(*args)


def on_device(query_rows, key_rows, value_rows, saved_out, out_grad, doc_lengths):
    shape = jax.ShapeDtypeStruct
    bf16, f32 = jnp.bfloat16, jnp.float32
    other = (swap_cores(key_rows), swap_cores(value_rows))
    mine = jnp.concatenate([key_rows, value_rows], axis=1)
    other, mine = lax.optimization_barrier((other, mine))
    own = call(pack_kernel, [shape((CHIP_ROWS, 2 * DH), bf16)])(mine, *other)[0]
    fetched = [move_chips(own, steps, 1) for steps in STEPS]
    prepared = call(
        prepare_kernel,
        [shape((COLS, DH), bf16), shape((COLS, DH), bf16), shape((8, COLS), f32), shape((WINDOW, DH), f32)],
        [pltpu.VMEM((ROWS, HQ * DH), bf16)] * 3
        + [pltpu.VMEM((1, 64), jnp.int32), pltpu.SemaphoreType.DMA((4,))],
        pl.ANY,
    )(query_rows, saved_out, out_grad, doc_lengths.reshape(1, 64))
    fetched, (q2, g2, row_dot, bias) = lax.optimization_barrier((fetched, prepared))
    near = jnp.concatenate(fetched, axis=0)
    far = swap_cores(near)
    keep, give, weights, grads = call(
        main_kernel,
        [shape((PAST // 2, 2 * DH), f32), shape((PAST // 2, 2 * DH), bf16),
         shape((WINDOW, COLS), bf16), shape((WINDOW, COLS), bf16)],
        [pltpu.VMEM((COLS // TILE, WINDOW // CHIP_ROWS, CHIP_ROWS, TILE), f32)],
    )(q2, g2, row_dot, bias, near, far, own)
    sums = (keep + swap_cores(give).astype(f32)).astype(bf16)
    back = [
        move_chips(sums[i * CHIP_ROWS : (i + 1) * CHIP_ROWS], steps, -1)
        for i, steps in enumerate(STEPS)
    ]
    query_grad, own_sums = call(
        finish_kernel,
        [shape((ROWS, HQ * DH), bf16), shape((CHIP_ROWS, 2 * DH), f32)],
    )(q2, g2, weights, grads, near, far, own)
    totals = own_sums + back[0].astype(f32) + back[1].astype(f32)
    result = totals[:ROWS] + swap_cores(totals[ROWS:].astype(bf16)).astype(f32)
    result = result.astype(bf16)
    return (query_grad, result[:, :DH], result[:, DH:])


def solution(mesh):
    placed = P(AXES, None)
    return jax.shard_map(
        on_device,
        mesh=mesh,
        in_specs=(placed,) * 5 + (P(),),
        out_specs=(placed,) * 3,
        check_vma=False,
    )
```

```python
import functools
import math

import jax
import jax.numpy as jnp
from jax import lax
from jax.experimental import pallas as pl
from jax.experimental.pallas import tpu as pltpu
from jax.sharding import PartitionSpec as P

DH = 128
HQ = 16
ROWS = 64
CHUNKS = 256
CHIPS = CHUNKS // 2
HALF_CHUNKS = 8
HALVES = CHUNKS // HALF_CHUNKS
COLS = HQ * ROWS
CHIP_ROWS = 2 * ROWS
PAST = 2 * CHIP_ROWS
TILE = 256
TILES = COLS // TILE
NEG = -1e30
SCALING = 1.0 / math.sqrt(DH)
EXP2_SCALING = SCALING * math.log2(math.e)
AXES = ("blk", "uly")
STEPS = ((1, 4), (2, 3))
CROSS = (1, 1)
PIECES = (0, 352, 704, COLS)
KEY_COLS, VALUE_COLS = slice(0, DH), slice(DH, 2 * DH)


def device_of(chunk):
    half, place = divmod(chunk, HALF_CHUNKS)
    if half < HALVES // 2:
        return half * 16 + place
    return (HALVES - 1 - half) * 16 + 8 + place


def swap_cores(x):
    return lax.ppermute(x, "uly", [(i, i ^ 1) for i in range(16)])


def move_chips(x, number, forward):
    steps, cross = STEPS[number], CROSS[number]
    pairs = []
    for chunk in range(CHUNKS):
        chip, core = divmod(chunk, 2)
        target = (chip + steps[core]) % CHIPS
        pair = (device_of(chunk), device_of(2 * target + (core ^ cross)))
        pairs.append(pair if forward else pair[::-1])
    return lax.ppermute(x, AXES, pairs)


def dot(a, b, contract):
    return lax.dot_general(a, b, (contract, ((), ())), preferred_element_type=jnp.float32)


def dot_nt(a, b):
    return dot(a, b, ((1,), (1,)))


def dot_nn(a, b):
    return dot(a, b, ((1,), (0,)))


def dot_tn(a, b):
    return dot(a, b, ((0,), (0,)))


def pack_kernel(mine_ref, other_k_ref, other_v_ref, w_ref):
    w_ref[:ROWS, :] = mine_ref[...]
    w_ref[ROWS:, :DH] = other_k_ref[...]
    w_ref[ROWS:, DH:] = other_v_ref[...]


def folded(x, op):
    return op(x.reshape(x.shape[0] // 8, 8, x.shape[1]), axis=0)


def tiles():
    for tile in range(2 * TILES):
        side, at = divmod(tile, TILES)
        yield slice(tile * TILE, (tile + 1) * TILE), side, slice(at * TILE, (at + 1) * TILE)


def scored(keys, query, bias):
    scores = dot_nt(keys, query) + jnp.concatenate([bias, bias], axis=1)
    top = jnp.max(folded(scores, jnp.max), axis=0, keepdims=True)
    weights = jnp.exp2((scores - top) * EXP2_SCALING)
    return weights, top, jnp.sum(folded(weights, jnp.sum), axis=0, keepdims=True)


def prepare_kernel(q_ref, o_ref, g_ref, partner_q_ref, partner_g_ref, len_ref, mine_ref,
                   q2_ref, g2_ref, dot_ref, bias_ref, e_ref, top_ref, sum_ref):
    blk = lax.axis_index("blk")
    uly = lax.axis_index("uly")
    core = lax.rem(uly, 2)
    place = lax.rem(uly, HALF_CHUNKS)
    half = jnp.where(uly < HALF_CHUNKS, blk, HALVES - 1 - blk)
    chunk = half * HALF_CHUNKS + place
    chip = chunk // 2

    ones = jnp.ones((8, DH), jnp.bfloat16)
    for h in range(HQ):
        cols = slice(h * DH, (h + 1) * DH)
        rows = slice(h * ROWS, (h + 1) * ROWS)
        grad = g_ref[:, cols]
        q2_ref[rows, :] = q_ref[:, cols]
        g2_ref[rows, :] = grad
        partner_rows = slice(COLS + h * ROWS, COLS + (h + 1) * ROWS)
        q2_ref[partner_rows, :] = partner_q_ref[:, cols]
        g2_ref[partner_rows, :] = partner_g_ref[:, cols]
        prod = grad.astype(jnp.float32) * o_ref[:, cols].astype(jnp.float32)
        high = prod.astype(jnp.bfloat16)
        low = (prod - high.astype(jnp.float32)).astype(jnp.bfloat16)
        dot_ref[:, rows] = (dot_nt(ones, high) + dot_nt(ones, low))[0:1]

    lens = jnp.broadcast_to(len_ref[...].astype(jnp.float32), (64, 64))
    doc = lax.broadcasted_iota(jnp.int32, (64, 64), 0)
    other = lax.broadcasted_iota(jnp.int32, (64, 64), 1)
    starts = jnp.sum(jnp.where(other < doc, lens, 0.0), axis=1, keepdims=True).astype(jnp.int32)
    lane = lax.broadcasted_iota(jnp.int32, (1, DH), 1)
    index = lax.broadcasted_iota(jnp.int32, (ROWS, DH), 0)
    chunks = []
    for steps, cross in zip(STEPS, CROSS):
        source = 1 - core if cross else core
        past = 2 * (chip - jnp.where(source == 0, steps[0], steps[1]))
        chunks += [past + source, past + 1 - source]
    own_bias = []
    for side in range(2):
        mine = chunk if side == 0 else 2 * chip + 1 - core
        here = mine * ROWS + lax.rem(lane, ROWS)
        first = jnp.max(jnp.where(starts <= here, starts, 0), axis=0, keepdims=True)

        def bias_of(key_chunk):
            where = key_chunk * ROWS + index
            return jnp.where((where >= first) & (where <= here), 0.0, NEG)

        for part, key_chunk in enumerate(chunks):
            at = side * PAST + part * ROWS
            bias_ref[at : at + ROWS, :] = bias_of(key_chunk)
        own_bias.append(bias_of(chunk))
    for cols, side, _ in tiles():
        e_ref[:, cols], top_ref[:, cols], sum_ref[:, cols] = scored(
            mine_ref[:, KEY_COLS], q2_ref[cols, :], own_bias[side]
        )


GROUPS = (slice(0, CHIP_ROWS), slice(CHIP_ROWS, PAST))


def score_kernel(q_ref, bias_ref, a_ref, b_ref, own_top_ref, own_sum_ref, e_ref, tops_ref, stats_ref):
    for cols, side, rows in tiles():
        query = q_ref[cols, :]
        tops, sums = [own_top_ref[:, cols]], [own_sum_ref[:, cols]]
        for i, (group, ref) in enumerate(zip(GROUPS, (a_ref, b_ref))):
            bias = bias_ref[side * PAST + group.start : side * PAST + group.stop, :]
            e_ref[group, cols], top, total = scored(ref[:, KEY_COLS], query, bias)
            tops_ref[i : i + 1, cols] = top
            tops.append(top)
            sums.append(total)
        most = functools.reduce(jnp.maximum, tops)
        stats_ref[2 * side : 2 * side + 1, rows] = most
        stats_ref[2 * side + 1 : 2 * side + 2, rows] = sum(
            x * jnp.exp2((top - most) * EXP2_SCALING) for x, top in zip(sums, tops)
        )


def slope_kernel(g_ref, dot_ref, partner_dot_ref, a_ref, b_ref, u_ref):
    for cols, side, rows in tiles():
        grad = g_ref[cols, :]
        row_dot = (dot_ref, partner_dot_ref)[side][:, rows]
        for group, ref in zip(GROUPS, (a_ref, b_ref)):
            u_ref[group, cols] = dot_nt(ref[:, VALUE_COLS], grad) - row_dot


def main_kernel(q_ref, g_ref, e_ref, u_ref, tops_ref, stats_ref, far_ref,
                a_ref, b_ref, ds_ref, norm_ref, p_ref):
    for cols, side, rows in tiles():
        near, far = 2 * side, 2 - 2 * side
        top = stats_ref[near : near + 1, rows]
        far_top = far_ref[far : far + 1, rows]
        most = jnp.maximum(top, far_top)
        total = stats_ref[near + 1 : near + 2, rows] * jnp.exp2(
            (top - most) * EXP2_SCALING
        ) + far_ref[far + 1 : far + 2, rows] * jnp.exp2((far_top - most) * EXP2_SCALING)
        norm_ref[0:1, cols] = most
        norm_ref[1:2, cols] = total
        for i, group in enumerate(GROUPS):
            factor = jnp.exp2((tops_ref[i : i + 1, cols] - most) * EXP2_SCALING) / total
            weights = e_ref[group, cols] * factor
            ds_ref[group, cols] = (weights * u_ref[group, cols]).astype(jnp.bfloat16)
            p_ref[group, cols] = weights.astype(jnp.bfloat16)
    for ref, group in zip((a_ref, b_ref), GROUPS):
        ref[:, KEY_COLS] = (dot_nn(ds_ref[group, :], q_ref[...]) * SCALING).astype(jnp.bfloat16)
        ref[:, VALUE_COLS] = dot_nn(p_ref[group, :], g_ref[...]).astype(jnp.bfloat16)


def finish_kernel(q_ref, g_ref, dot_ref, partner_dot_ref, own_e_ref, own_top_ref, norm_ref, ds_ref,
                  mine_ref, a_ref, b_ref, dq_ref, own_ref, *rest):
    *piece_refs, own_p_ref, own_ds_ref = rest
    past_keys = jnp.concatenate([a_ref[:, KEY_COLS], b_ref[:, KEY_COLS]], axis=0)
    for cols, side, rows in reversed(list(tiles())):
        row_dot = (dot_ref, partner_dot_ref)[side][:, rows]
        slopes = dot_nt(mine_ref[:, VALUE_COLS], g_ref[cols, :]) - row_dot
        factor = jnp.exp2((own_top_ref[:, cols] - norm_ref[0:1, cols]) * EXP2_SCALING)
        weights = own_e_ref[:, cols] * (factor / norm_ref[1:2, cols])
        own_ds = (weights * slopes).astype(jnp.bfloat16)
        own_p_ref[:, cols] = weights.astype(jnp.bfloat16)
        own_ds_ref[:, cols] = own_ds
        grads = (dot_tn(past_keys, ds_ref[:, cols]) + dot_tn(mine_ref[:, KEY_COLS], own_ds)) * SCALING
        for j in range(TILE // DH):
            pair = grads[:, j * DH : (j + 1) * DH].T
            at = rows.start + j * DH
            if side == 0:
                dq_ref[at : at + DH, :] = pair
                continue
            for start, ref in zip(PIECES, piece_refs):
                low, high = max(at, start), min(at + DH, start + ref.shape[0])
                if low < high:
                    ref[low - start : high - start, :] = pair[low - at : high - at].astype(jnp.bfloat16)
    own_ref[:, KEY_COLS] = dot_nn(own_ds_ref[...], q_ref[...]) * SCALING
    own_ref[:, VALUE_COLS] = dot_nn(own_p_ref[...], g_ref[...])


def add_kernel(dq_ref, *refs):
    *piece_refs, sum_ref = refs
    for h in range(HQ):
        total = dq_ref[h * ROWS : (h + 1) * ROWS, :]
        low = h * ROWS
        parts = []
        for start, ref in zip(PIECES, piece_refs):
            first, last = max(low, start), min(low + ROWS, start + ref.shape[0])
            if first < last:
                parts.append(ref[first - start : last - start, :].astype(jnp.float32))
        partner = parts[0] if len(parts) == 1 else jnp.concatenate(parts, axis=0)
        sum_ref[:, h * DH : (h + 1) * DH] = (total + partner).astype(jnp.bfloat16)


def call(kernel, outs, scratch=(), flops=10**9):
    vmem = pl.BlockSpec(memory_space=pltpu.VMEM)
    return lambda *args: pl.pallas_call(
        kernel,
        out_shape=outs,
        in_specs=[vmem] * len(args),
        out_specs=[vmem] * len(outs),
        scratch_shapes=list(scratch),
        compiler_params=pltpu.CompilerParams(vmem_limit_bytes=24 * 1024 * 1024),
        cost_estimate=pl.CostEstimate(flops=flops, bytes_accessed=flops // 500, transcendentals=0),
    )(*args)


def on_device(query_rows, key_rows, value_rows, saved_out, out_grad, doc_lengths):
    shape = jax.ShapeDtypeStruct
    bf16, f32 = jnp.bfloat16, jnp.float32
    together = lax.optimization_barrier
    other = (swap_cores(key_rows), swap_cores(value_rows))
    partner = (swap_cores(query_rows), swap_cores(out_grad))
    mine = jnp.concatenate([key_rows, value_rows], axis=1)
    other, mine = together((other, mine))
    own = call(pack_kernel, [shape((CHIP_ROWS, 2 * DH), bf16)])(mine, *other)[0]
    fetched = [move_chips(own, number, True) for number in range(2)]
    columns = 2 * COLS
    prepared = call(
        prepare_kernel,
        [shape((columns, DH), bf16), shape((columns, DH), bf16), shape((1, COLS), f32),
         shape((2 * PAST, DH), f32), shape((ROWS, columns), f32), shape((1, columns), f32),
         shape((1, columns), f32)],
    )(query_rows, saved_out, out_grad, *partner, doc_lengths.reshape(1, 64), mine)
    far_dot = swap_cores(prepared[2])
    fetched, far_dot, prepared = together((fetched, far_dot, prepared))
    q2, g2, row_dot, bias, own_weights, own_top, own_sum = prepared
    weights, tops, stats = call(
        score_kernel, [shape((PAST, columns), f32), shape((2, columns), f32), shape((4, COLS), f32)]
    )(q2, bias, *fetched, own_top, own_sum)
    far_stats = swap_cores(stats)
    slopes = call(slope_kernel, [shape((PAST, columns), f32)])(g2, row_dot, far_dot, *fetched)[0]
    far_stats, slopes = together((far_stats, slopes))
    part_a, part_b, ds, norm = call(
        main_kernel,
        [shape((CHIP_ROWS, 2 * DH), bf16), shape((CHIP_ROWS, 2 * DH), bf16),
         shape((PAST, columns), bf16), shape((2, columns), f32)],
        [pltpu.VMEM((PAST, columns), bf16)],
    )(q2, g2, weights, slopes, tops, stats, far_stats)
    back = [move_chips(part, number, False) for number, part in enumerate((part_a, part_b))]
    query_grad, own_sums, *pieces = call(
        finish_kernel,
        [shape((COLS, DH), f32), shape((ROWS, 2 * DH), f32)]
        + [shape((high - low, DH), bf16) for low, high in zip(PIECES, PIECES[1:])],
        [pltpu.VMEM((ROWS, columns), bf16)] * 2,
    )(q2, g2, row_dot, far_dot, own_weights, own_top, norm, ds, mine, *fetched)
    pieces = [swap_cores(piece) for piece in pieces]
    totals = back[1].astype(f32) + back[0].astype(f32)
    far_totals = swap_cores(totals[ROWS:].astype(bf16))
    totals, query_grad = together((totals, query_grad))
    query_grad = call(add_kernel, [shape((ROWS, HQ * DH), bf16)])(query_grad, *pieces)[0]
    far_totals, query_grad = together((far_totals, query_grad))
    result = totals[:ROWS] + own_sums + far_totals.astype(f32)
    result = result.astype(bf16)
    return (query_grad, result[:, :DH], result[:, DH:])


def solution(mesh):
    placed = P(AXES, None)
    return jax.shard_map(
        on_device,
        mesh=mesh,
        in_specs=(placed,) * 5 + (P(),),
        out_specs=(placed,) * 3,
        check_vma=False,
    )
```

```python
import functools
import math

import jax
import jax.numpy as jnp
from jax import lax
from jax.experimental import pallas as pl
from jax.experimental.pallas import tpu as pltpu
from jax.sharding import PartitionSpec as P

DH = 128
HQ = 16
ROWS = 64
CHUNKS = 256
CHIPS = CHUNKS // 2
HALF_CHUNKS = 8
HALVES = CHUNKS // HALF_CHUNKS
COLS = HQ * ROWS
CHIP_ROWS = 2 * ROWS
PAST = 2 * CHIP_ROWS
TILE = 256
TILES = COLS // TILE
NEG = -1e30
SCALING = 1.0 / math.sqrt(DH)
EXP2_SCALING = SCALING * math.log2(math.e)
AXES = ("blk", "uly")
STEPS = ((1, 4), (2, 3))
CROSS = (1, 1)
PIECES = (0, 352, 704, COLS)
KEY_COLS, VALUE_COLS = slice(0, DH), slice(DH, 2 * DH)


def device_of(chunk):
    half, place = divmod(chunk, HALF_CHUNKS)
    if half < HALVES // 2:
        return half * 16 + place
    return (HALVES - 1 - half) * 16 + 8 + place


def swap_cores(x):
    return lax.ppermute(x, "uly", [(i, i ^ 1) for i in range(16)])


def move_chips(x, number, forward):
    steps, cross = STEPS[number], CROSS[number]
    pairs = []
    for chunk in range(CHUNKS):
        chip, core = divmod(chunk, 2)
        target = (chip + steps[core]) % CHIPS
        pair = (device_of(chunk), device_of(2 * target + (core ^ cross)))
        pairs.append(pair if forward else pair[::-1])
    return lax.ppermute(x, AXES, pairs)


def dot(a, b, contract):
    return lax.dot_general(a, b, (contract, ((), ())), preferred_element_type=jnp.float32)


def dot_nt(a, b):
    return dot(a, b, ((1,), (1,)))


def dot_nn(a, b):
    return dot(a, b, ((1,), (0,)))


def dot_tn(a, b):
    return dot(a, b, ((0,), (0,)))


def pack_kernel(mine_ref, other_k_ref, other_v_ref, w_ref):
    w_ref[:ROWS, :] = mine_ref[...]
    w_ref[ROWS:, :DH] = other_k_ref[...]
    w_ref[ROWS:, DH:] = other_v_ref[...]


def folded(x, op):
    return op(x.reshape(x.shape[0] // 8, 8, x.shape[1]), axis=0)


def tiles():
    for tile in range(2 * TILES):
        side, at = divmod(tile, TILES)
        yield slice(tile * TILE, (tile + 1) * TILE), side, slice(at * TILE, (at + 1) * TILE)


def query_tile(queries, side):
    row = lax.rem(lax.broadcasted_iota(jnp.int32, (TILE, DH), 0), ROWS) + side * ROWS
    lane = lax.broadcasted_iota(jnp.int32, (TILE, DH), 1)
    return jnp.concatenate([queries, (row == lane).astype(jnp.bfloat16)], axis=1)


def scored(scores):
    top = jnp.max(folded(scores, jnp.max), axis=0, keepdims=True)
    weights = jnp.exp2((scores - top) * EXP2_SCALING)
    return weights, top, jnp.sum(folded(weights, jnp.sum), axis=0, keepdims=True)


def prepare_kernel(q_ref, o_ref, g_ref, len_ref, own_ref,
                   q2_ref, g2_ref, dot_ref, bias_ref, e_ref, top_ref, sum_ref):
    blk = lax.axis_index("blk")
    uly = lax.axis_index("uly")
    core = lax.rem(uly, 2)
    place = lax.rem(uly, HALF_CHUNKS)
    half = jnp.where(uly < HALF_CHUNKS, blk, HALVES - 1 - blk)
    chunk = half * HALF_CHUNKS + place
    chip = chunk // 2

    ones = jnp.ones((8, DH), jnp.bfloat16)
    for h in range(HQ):
        cols = slice(h * DH, (h + 1) * DH)
        rows = slice(h * ROWS, (h + 1) * ROWS)
        grad = g_ref[:, cols]
        q2_ref[rows, :] = q_ref[:, cols]
        g2_ref[rows, :] = grad
        prod = grad.astype(jnp.float32) * o_ref[:, cols].astype(jnp.float32)
        high = prod.astype(jnp.bfloat16)
        low = (prod - high.astype(jnp.float32)).astype(jnp.bfloat16)
        dot_ref[:, rows] = (dot_nt(ones, high) + dot_nt(ones, low))[0:1]

    lens = jnp.broadcast_to(len_ref[...].astype(jnp.float32), (64, 64))
    doc = lax.broadcasted_iota(jnp.int32, (64, 64), 0)
    other = lax.broadcasted_iota(jnp.int32, (64, 64), 1)
    starts = jnp.sum(jnp.where(other < doc, lens, 0.0), axis=1, keepdims=True).astype(jnp.int32)
    lane = lax.broadcasted_iota(jnp.int32, (1, DH), 1)
    here = jnp.where(lane < ROWS, chunk, 2 * chip + 1 - core) * ROWS + lax.rem(lane, ROWS)
    first = jnp.max(jnp.where(starts <= here, starts, 0), axis=0, keepdims=True)
    index = lax.broadcasted_iota(jnp.int32, (ROWS, DH), 0)
    chunks = []
    for steps, cross in zip(STEPS, CROSS):
        source = 1 - core if cross else core
        past = 2 * (chip - jnp.where(source == 0, steps[0], steps[1]))
        chunks += [past + source, past + 1 - source]
    for part, key_chunk in enumerate(chunks + [chunk, 2 * chip + 1 - core]):
        where = key_chunk * ROWS + index
        bias = jnp.where((where >= first) & (where <= here), 0.0, NEG).astype(jnp.bfloat16)
        bias_ref[part * ROWS : (part + 1) * ROWS, :] = bias
    keys = jnp.concatenate([own_ref[:, KEY_COLS], bias_ref[PAST:, :]], axis=1)
    for tile in range(TILES):
        cols = slice(tile * TILE, (tile + 1) * TILE)
        e_ref[:, cols], top_ref[:, cols], sum_ref[:, cols] = scored(
            dot_nt(keys, query_tile(q2_ref[cols, :], 0))
        )


def keys_kernel(a_ref, b_ref, bias_ref, keys_ref):
    for ref, group in zip((a_ref, b_ref), GROUPS):
        keys_ref[group, :DH] = ref[:, KEY_COLS]
    keys_ref[:, DH:] = bias_ref[:PAST, :]


GROUPS = (slice(0, CHIP_ROWS), slice(CHIP_ROWS, PAST))


def score_kernel(q_ref, partner_q_ref, keys_ref, own_top_ref, own_sum_ref,
                 e_ref, tops_ref, stats_ref):
    for cols, side, rows in tiles():
        query = query_tile((q_ref, partner_q_ref)[side][rows, :], side)
        scores = dot_nt(keys_ref[...], query)
        tops, sums = [], []
        for i, group in enumerate(GROUPS):
            e_ref[group, cols], top, total = scored(scores[group])
            tops_ref[i : i + 1, cols] = top
            tops.append(top)
            sums.append(total)
        if side == 0:
            tops.append(own_top_ref[:, rows])
            sums.append(own_sum_ref[:, rows])
        most = functools.reduce(jnp.maximum, tops)
        stats_ref[2 * side : 2 * side + 1, rows] = most
        stats_ref[2 * side + 1 : 2 * side + 2, rows] = sum(
            x * jnp.exp2((top - most) * EXP2_SCALING) for x, top in zip(sums, tops)
        )


def slope_kernel(g_ref, partner_g_ref, dot_ref, partner_dot_ref, a_ref, b_ref, u_ref):
    values = jnp.concatenate([a_ref[:, VALUE_COLS], b_ref[:, VALUE_COLS]], axis=0)
    for cols, side, rows in tiles():
        grad = (g_ref, partner_g_ref)[side][rows, :]
        u_ref[:, cols] = dot_nt(values, grad) - (dot_ref, partner_dot_ref)[side][:, rows]


def dot_sides(left_ref, own_ref, partner_ref):
    return dot_nn(left_ref[:, :COLS], own_ref[...]) + dot_nn(left_ref[:, COLS:], partner_ref[...])


def main_kernel(q_ref, partner_q_ref, g_ref, partner_g_ref, e_ref, u_ref, tops_ref, stats_ref, far_ref,
                a_ref, b_ref, ds_ref, norm_ref, p_ref):
    for cols, side, rows in tiles():
        near, far = 2 * side, 2 - 2 * side
        top = stats_ref[near : near + 1, rows]
        far_top = far_ref[far : far + 1, rows]
        most = jnp.maximum(top, far_top)
        total = stats_ref[near + 1 : near + 2, rows] * jnp.exp2(
            (top - most) * EXP2_SCALING
        ) + far_ref[far + 1 : far + 2, rows] * jnp.exp2((far_top - most) * EXP2_SCALING)
        norm_ref[0:1, cols] = most
        norm_ref[1:2, cols] = total
        for i, group in enumerate(GROUPS):
            factor = jnp.exp2((tops_ref[i : i + 1, cols] - most) * EXP2_SCALING) / total
            weights = e_ref[group, cols] * factor
            ds_ref[group, cols] = (weights * u_ref[group, cols]).astype(jnp.bfloat16)
            p_ref[group, cols] = weights.astype(jnp.bfloat16)
    key_grads = (dot_sides(ds_ref, q_ref, partner_q_ref) * SCALING).astype(jnp.bfloat16)
    value_grads = dot_sides(p_ref, g_ref, partner_g_ref).astype(jnp.bfloat16)
    for ref, group in zip((a_ref, b_ref), GROUPS):
        ref[:, KEY_COLS] = key_grads[group]
        ref[:, VALUE_COLS] = value_grads[group]


def finish_kernel(q_ref, g_ref, dot_ref, own_e_ref, own_top_ref, norm_ref, ds_ref, own_ref, a_ref, b_ref,
                  dq_ref, own_sum_ref, *rest):
    *piece_refs, own_p_ref, own_ds_ref = rest
    past_keys = jnp.concatenate([a_ref[:, KEY_COLS], b_ref[:, KEY_COLS]], axis=0)
    for cols, side, rows in reversed(list(tiles())):
        grads = dot_tn(past_keys, ds_ref[:, cols])
        if side == 0:
            slopes = dot_nt(own_ref[:, VALUE_COLS], g_ref[rows, :]) - dot_ref[:, rows]
            factor = jnp.exp2((own_top_ref[:, rows] - norm_ref[0:1, rows]) * EXP2_SCALING)
            weights = own_e_ref[:, rows] * (factor / norm_ref[1:2, rows])
            own_ds = (weights * slopes).astype(jnp.bfloat16)
            own_p_ref[:, rows] = weights.astype(jnp.bfloat16)
            own_ds_ref[:, rows] = own_ds
            grads = grads + dot_tn(own_ref[:, KEY_COLS], own_ds)
        grads = grads * SCALING
        for j in range(TILE // DH):
            pair = grads[:, j * DH : (j + 1) * DH].T
            at = rows.start + j * DH
            if side == 0:
                dq_ref[at : at + DH, :] = pair
                continue
            for start, ref in zip(PIECES, piece_refs):
                low, high = max(at, start), min(at + DH, start + ref.shape[0])
                if low < high:
                    ref[low - start : high - start, :] = pair[low - at : high - at].astype(jnp.bfloat16)
    own_sum_ref[:, KEY_COLS] = dot_nn(own_ds_ref[...], q_ref[...]) * SCALING
    own_sum_ref[:, VALUE_COLS] = dot_nn(own_p_ref[...], g_ref[...])


def add_kernel(dq_ref, *refs):
    *piece_refs, sum_ref = refs
    for h in range(HQ):
        total = dq_ref[h * ROWS : (h + 1) * ROWS, :]
        low = h * ROWS
        parts = []
        for start, ref in zip(PIECES, piece_refs):
            first, last = max(low, start), min(low + ROWS, start + ref.shape[0])
            if first < last:
                parts.append(ref[first - start : last - start, :].astype(jnp.float32))
        partner = parts[0] if len(parts) == 1 else jnp.concatenate(parts, axis=0)
        sum_ref[:, h * DH : (h + 1) * DH] = (total + partner).astype(jnp.bfloat16)


def call(kernel, outs, scratch=(), flops=10**9):
    vmem = pl.BlockSpec(memory_space=pltpu.VMEM)
    return lambda *args: pl.pallas_call(
        kernel,
        out_shape=outs,
        in_specs=[vmem] * len(args),
        out_specs=[vmem] * len(outs),
        scratch_shapes=list(scratch),
        compiler_params=pltpu.CompilerParams(vmem_limit_bytes=24 * 1024 * 1024),
        cost_estimate=pl.CostEstimate(flops=flops, bytes_accessed=flops // 500, transcendentals=0),
    )(*args)


def on_device(query_rows, key_rows, value_rows, saved_out, out_grad, doc_lengths):
    shape = jax.ShapeDtypeStruct
    bf16, f32 = jnp.bfloat16, jnp.float32
    together = lax.optimization_barrier
    other = (swap_cores(key_rows), swap_cores(value_rows))
    mine = jnp.concatenate([key_rows, value_rows], axis=1)
    other, mine = together((other, mine))
    own = call(pack_kernel, [shape((CHIP_ROWS, 2 * DH), bf16)])(mine, *other)[0]
    fetched = [move_chips(own, number, True) for number in range(2)]
    columns = 2 * COLS
    q2, g2, row_dot, bias, own_weights, own_top, own_sum = call(
        prepare_kernel,
        [shape((COLS, DH), bf16), shape((COLS, DH), bf16), shape((1, COLS), f32),
         shape((PAST + CHIP_ROWS, DH), bf16), shape((CHIP_ROWS, COLS), f32), shape((1, COLS), f32),
         shape((1, COLS), f32)],
    )(query_rows, saved_out, out_grad, doc_lengths.reshape(1, 64), own)
    keys = call(keys_kernel, [shape((PAST, 2 * DH), bf16)], flops=3 * 10**9)(*fetched, bias)[0]
    q3, g3, far_dot = (swap_cores(x) for x in (q2, g2, row_dot))
    weights, tops, stats = call(
        score_kernel, [shape((PAST, columns), f32), shape((2, columns), f32), shape((4, COLS), f32)]
    )(q2, q3, keys, own_top, own_sum)
    far_stats = swap_cores(stats)
    slopes = call(slope_kernel, [shape((PAST, columns), f32)])(
        g2, g3, row_dot, far_dot, *fetched
    )[0]
    far_stats, slopes = together((far_stats, slopes))
    part_a, part_b, ds, norm = call(
        main_kernel,
        [shape((CHIP_ROWS, 2 * DH), bf16), shape((CHIP_ROWS, 2 * DH), bf16),
         shape((PAST, columns), bf16), shape((2, columns), f32)],
        [pltpu.VMEM((PAST, columns), bf16)],
    )(q2, q3, g2, g3, weights, slopes, tops, stats, far_stats)
    back = [move_chips(part, number, False) for number, part in enumerate((part_a, part_b))]
    query_grad, own_sums, *pieces = call(
        finish_kernel,
        [shape((COLS, DH), f32), shape((CHIP_ROWS, 2 * DH), f32)]
        + [shape((high - low, DH), bf16) for low, high in zip(PIECES, PIECES[1:])],
        [pltpu.VMEM((CHIP_ROWS, COLS), bf16)] * 2,
    )(q2, g2, row_dot, own_weights, own_top, norm, ds, own, *fetched)
    pieces = [swap_cores(piece) for piece in pieces]
    totals = back[1].astype(f32) + back[0].astype(f32) + own_sums
    far_totals = swap_cores(totals[ROWS:].astype(bf16))
    totals, query_grad = together((totals, query_grad))
    query_grad = call(add_kernel, [shape((ROWS, HQ * DH), bf16)])(query_grad, *pieces)[0]
    far_totals, query_grad = together((far_totals, query_grad))
    result = totals[:ROWS] + far_totals.astype(f32)
    result = result.astype(bf16)
    return (query_grad, result[:, :DH], result[:, DH:])


def solution(mesh):
    placed = P(AXES, None)
    return jax.shard_map(
        on_device,
        mesh=mesh,
        in_specs=(placed,) * 5 + (P(),),
        out_specs=(placed,) * 3,
        check_vma=False,
    )
```

```python
import functools
import math

import jax
import jax.numpy as jnp
from jax import lax
from jax.experimental import pallas as pl
from jax.experimental.pallas import tpu as pltpu
from jax.sharding import PartitionSpec as P

DH = 128
HQ = 16
ROWS = 64
CHUNKS = 256
CHIPS = CHUNKS // 2
HALF_CHUNKS = 8
HALVES = CHUNKS // HALF_CHUNKS
COLS = HQ * ROWS
CHIP_ROWS = 2 * ROWS
PAST = 2 * CHIP_ROWS
TILE = 256
TILES = COLS // TILE
NEG = -1e30
SCALING = 1.0 / math.sqrt(DH)
EXP2_SCALING = SCALING * math.log2(math.e)
AXES = ("blk", "uly")
STEPS = ((1, 4), (3, 2))
CROSS = (1, 1)
PIECES = (0, 352, 704, COLS)
KEY_COLS, VALUE_COLS = slice(0, DH), slice(DH, 2 * DH)


def device_of(chunk):
    half, place = divmod(chunk, HALF_CHUNKS)
    if half < HALVES // 2:
        return half * 16 + place
    return (HALVES - 1 - half) * 16 + 8 + place


def swap_cores(x):
    return lax.ppermute(x, "uly", [(i, i ^ 1) for i in range(16)])


def move_chips(x, number, forward):
    steps, cross = STEPS[number], CROSS[number]
    pairs = []
    for chunk in range(CHUNKS):
        chip, core = divmod(chunk, 2)
        target = (chip + steps[core]) % CHIPS
        pair = (device_of(chunk), device_of(2 * target + (core ^ cross)))
        pairs.append(pair if forward else pair[::-1])
    return lax.ppermute(x, AXES, pairs)


def dot(a, b, contract):
    return lax.dot_general(a, b, (contract, ((), ())), preferred_element_type=jnp.float32)


def dot_nt(a, b):
    return dot(a, b, ((1,), (1,)))


def dot_nn(a, b):
    return dot(a, b, ((1,), (0,)))


def dot_tn(a, b):
    return dot(a, b, ((0,), (0,)))


def pack_kernel(mine_ref, other_k_ref, other_v_ref, w_ref):
    w_ref[:ROWS, :] = mine_ref[...]
    w_ref[ROWS:, :DH] = other_k_ref[...]
    w_ref[ROWS:, DH:] = other_v_ref[...]


def folded(x, op):
    return op(x.reshape(x.shape[0] // 8, 8, x.shape[1]), axis=0)


def tiles():
    for tile in range(2 * TILES):
        side, at = divmod(tile, TILES)
        yield slice(tile * TILE, (tile + 1) * TILE), side, slice(at * TILE, (at + 1) * TILE)


def query_tile(queries, side):
    row = lax.rem(lax.broadcasted_iota(jnp.int32, (DH, DH), 0), ROWS) + side * ROWS
    lane = lax.broadcasted_iota(jnp.int32, (DH, DH), 1)
    hot = (row == lane).astype(jnp.bfloat16)
    return jnp.concatenate([queries, jnp.concatenate([hot] * (queries.shape[0] // DH), axis=0)], axis=1)


def scored(scores):
    top = jnp.max(folded(scores, jnp.max), axis=0, keepdims=True)
    weights = jnp.exp2((scores - top) * EXP2_SCALING)
    return weights, top, jnp.sum(folded(weights, jnp.sum), axis=0, keepdims=True)


def prepare_kernel(q_ref, o_ref, g_ref, len_ref, own_ref,
                   q2_ref, g2_ref, dot_ref, bias_ref, e_ref, top_ref, sum_ref):
    blk = lax.axis_index("blk")
    uly = lax.axis_index("uly")
    core = lax.rem(uly, 2)
    place = lax.rem(uly, HALF_CHUNKS)
    half = jnp.where(uly < HALF_CHUNKS, blk, HALVES - 1 - blk)
    chunk = half * HALF_CHUNKS + place
    chip = chunk // 2

    ones = jnp.ones((8, DH), jnp.bfloat16)
    for h in range(HQ):
        cols = slice(h * DH, (h + 1) * DH)
        rows = slice(h * ROWS, (h + 1) * ROWS)
        grad = g_ref[:, cols]
        q2_ref[rows, :] = q_ref[:, cols]
        g2_ref[rows, :] = grad
        prod = grad.astype(jnp.float32) * o_ref[:, cols].astype(jnp.float32)
        high = prod.astype(jnp.bfloat16)
        low = (prod - high.astype(jnp.float32)).astype(jnp.bfloat16)
        dot_ref[:, rows] = (dot_nt(ones, high) + dot_nt(ones, low))[0:1]

    lens = jnp.broadcast_to(len_ref[...].astype(jnp.float32), (64, 64))
    doc = lax.broadcasted_iota(jnp.int32, (64, 64), 0)
    other = lax.broadcasted_iota(jnp.int32, (64, 64), 1)
    starts = jnp.sum(jnp.where(other < doc, lens, 0.0), axis=1, keepdims=True).astype(jnp.int32)
    lane = lax.broadcasted_iota(jnp.int32, (1, DH), 1)
    here = jnp.where(lane < ROWS, chunk, 2 * chip + 1 - core) * ROWS + lax.rem(lane, ROWS)
    first = jnp.max(jnp.where(starts <= here, starts, 0), axis=0, keepdims=True)
    index = lax.broadcasted_iota(jnp.int32, (ROWS, DH), 0)
    chunks = []
    for steps, cross in zip(STEPS, CROSS):
        source = 1 - core if cross else core
        past = 2 * (chip - jnp.where(source == 0, steps[0], steps[1]))
        chunks += [past + source, past + 1 - source]
    for part, key_chunk in enumerate(chunks + [chunk, 2 * chip + 1 - core]):
        where = key_chunk * ROWS + index
        bias = jnp.where((where >= first) & (where <= here), 0.0, NEG).astype(jnp.bfloat16)
        bias_ref[part * ROWS : (part + 1) * ROWS, :] = bias
    keys = jnp.concatenate([own_ref[:, KEY_COLS], bias_ref[PAST:, :]], axis=1)
    for tile in range(TILES):
        cols = slice(tile * TILE, (tile + 1) * TILE)
        e_ref[:, cols], top_ref[:, cols], sum_ref[:, cols] = scored(
            dot_nt(keys, query_tile(q2_ref[cols, :], 0))
        )


def keys_kernel(a_ref, b_ref, bias_ref, keys_ref):
    for ref, group in zip((a_ref, b_ref), GROUPS):
        keys_ref[group, :DH] = ref[:, KEY_COLS]
    keys_ref[:, DH:] = bias_ref[:PAST, :]


GROUPS = (slice(0, CHIP_ROWS), slice(CHIP_ROWS, PAST))


def score_kernel(q_ref, partner_q_ref, keys_ref, own_top_ref, own_sum_ref,
                 e_ref, tops_ref, stats_ref):
    for side, ref in enumerate((q_ref, partner_q_ref)):
        e_ref[:, side * COLS : (side + 1) * COLS] = dot_nt(keys_ref[...], query_tile(ref[...], side))
    for at in range(0, 2 * COLS, DH):
        side, start = divmod(at, COLS)
        cols, rows = slice(at, at + DH), slice(start, start + DH)
        tops, sums = [], []
        for i, group in enumerate(GROUPS):
            e_ref[group, cols], top, total = scored(e_ref[group, cols])
            tops_ref[i : i + 1, cols] = top
            tops.append(top)
            sums.append(total)
        if side == 0:
            tops.append(own_top_ref[:, rows])
            sums.append(own_sum_ref[:, rows])
        most = functools.reduce(jnp.maximum, tops)
        stats_ref[2 * side : 2 * side + 1, rows] = most
        stats_ref[2 * side + 1 : 2 * side + 2, rows] = sum(
            x * jnp.exp2((top - most) * EXP2_SCALING) for x, top in zip(sums, tops)
        )


def slope_kernel(g_ref, partner_g_ref, dot_ref, partner_dot_ref, a_ref, b_ref, u_ref):
    values = jnp.concatenate([a_ref[:, VALUE_COLS], b_ref[:, VALUE_COLS]], axis=0)
    for cols, side, rows in tiles():
        grad = (g_ref, partner_g_ref)[side][rows, :]
        u_ref[:, cols] = dot_nt(values, grad) - (dot_ref, partner_dot_ref)[side][:, rows]


def dot_sides(left_ref, own_ref, partner_ref):
    return dot_nn(left_ref[:, :COLS], own_ref[...]) + dot_nn(left_ref[:, COLS:], partner_ref[...])


def main_kernel(q_ref, partner_q_ref, g_ref, partner_g_ref, e_ref, u_ref, tops_ref, stats_ref, far_ref,
                a_ref, b_ref, ds_ref, norm_ref, p_ref):
    for side in range(2):
        near, far = 2 * side, 2 - 2 * side
        top, far_top = stats_ref[near : near + 1, :], far_ref[far : far + 1, :]
        most = jnp.maximum(top, far_top)
        total = stats_ref[near + 1 : near + 2, :] * jnp.exp2(
            (top - most) * EXP2_SCALING
        ) + far_ref[far + 1 : far + 2, :] * jnp.exp2((far_top - most) * EXP2_SCALING)
        columns = slice(side * COLS, (side + 1) * COLS)
        norm_ref[0:1, columns] = most
        norm_ref[1:2, columns] = total
        factors = jnp.exp2((tops_ref[:, columns] - most) * EXP2_SCALING) * (1.0 / total)
        for start in range(0, COLS, TILE):
            cols = slice(side * COLS + start, side * COLS + start + TILE)
            for i, group in enumerate(GROUPS):
                weights = e_ref[group, cols] * factors[i : i + 1, start : start + TILE]
                ds_ref[group, cols] = (weights * u_ref[group, cols]).astype(jnp.bfloat16)
                p_ref[group, cols] = weights.astype(jnp.bfloat16)
    key_grads = (dot_sides(ds_ref, q_ref, partner_q_ref) * SCALING).astype(jnp.bfloat16)
    value_grads = dot_sides(p_ref, g_ref, partner_g_ref).astype(jnp.bfloat16)
    for ref, group in zip((a_ref, b_ref), GROUPS):
        ref[:, KEY_COLS] = key_grads[group]
        ref[:, VALUE_COLS] = value_grads[group]


def finish_kernel(q_ref, g_ref, dot_ref, own_e_ref, own_top_ref, norm_ref, ds_ref, own_ref, a_ref, b_ref,
                  dq_ref, own_sum_ref, *rest):
    *piece_refs, own_p_ref, own_ds_ref = rest
    past_keys = jnp.concatenate([a_ref[:, KEY_COLS], b_ref[:, KEY_COLS]], axis=0)
    for cols, side, rows in reversed(list(tiles())):
        grads = dot_tn(past_keys, ds_ref[:, cols])
        if side == 0:
            slopes = dot_nt(own_ref[:, VALUE_COLS], g_ref[rows, :]) - dot_ref[:, rows]
            factor = jnp.exp2((own_top_ref[:, rows] - norm_ref[0:1, rows]) * EXP2_SCALING)
            weights = own_e_ref[:, rows] * (factor / norm_ref[1:2, rows])
            own_ds = (weights * slopes).astype(jnp.bfloat16)
            own_p_ref[:, rows] = weights.astype(jnp.bfloat16)
            own_ds_ref[:, rows] = own_ds
            grads = grads + dot_tn(own_ref[:, KEY_COLS], own_ds)
        grads = grads * SCALING
        for j in range(TILE // DH):
            pair = grads[:, j * DH : (j + 1) * DH].T
            at = rows.start + j * DH
            if side == 0:
                dq_ref[at : at + DH, :] = pair
                continue
            for start, ref in zip(PIECES, piece_refs):
                low, high = max(at, start), min(at + DH, start + ref.shape[0])
                if low < high:
                    ref[low - start : high - start, :] = pair[low - at : high - at].astype(jnp.bfloat16)
    own_sum_ref[:, KEY_COLS] = dot_nn(own_ds_ref[...], q_ref[...]) * SCALING
    own_sum_ref[:, VALUE_COLS] = dot_nn(own_p_ref[...], g_ref[...])


def add_kernel(dq_ref, *refs):
    *piece_refs, sum_ref = refs
    for h in range(HQ):
        total = dq_ref[h * ROWS : (h + 1) * ROWS, :]
        low = h * ROWS
        parts = []
        for start, ref in zip(PIECES, piece_refs):
            first, last = max(low, start), min(low + ROWS, start + ref.shape[0])
            if first < last:
                parts.append(ref[first - start : last - start, :].astype(jnp.float32))
        partner = parts[0] if len(parts) == 1 else jnp.concatenate(parts, axis=0)
        sum_ref[:, h * DH : (h + 1) * DH] = (total + partner).astype(jnp.bfloat16)


def call(kernel, outs, scratch=(), flops=10**9):
    vmem = pl.BlockSpec(memory_space=pltpu.VMEM)
    return lambda *args: pl.pallas_call(
        kernel,
        out_shape=outs,
        in_specs=[vmem] * len(args),
        out_specs=[vmem] * len(outs),
        scratch_shapes=list(scratch),
        compiler_params=pltpu.CompilerParams(vmem_limit_bytes=24 * 1024 * 1024),
        cost_estimate=pl.CostEstimate(flops=flops, bytes_accessed=flops // 500, transcendentals=0),
    )(*args)


def on_device(query_rows, key_rows, value_rows, saved_out, out_grad, doc_lengths):
    shape = jax.ShapeDtypeStruct
    bf16, f32 = jnp.bfloat16, jnp.float32
    together = lax.optimization_barrier
    other = (swap_cores(key_rows), swap_cores(value_rows))
    mine = jnp.concatenate([key_rows, value_rows], axis=1)
    other, mine = together((other, mine))
    own = call(pack_kernel, [shape((CHIP_ROWS, 2 * DH), bf16)])(mine, *other)[0]
    fetched = [move_chips(own, number, True) for number in range(2)]
    columns = 2 * COLS
    q2, g2, row_dot, bias, own_weights, own_top, own_sum = call(
        prepare_kernel,
        [shape((COLS, DH), bf16), shape((COLS, DH), bf16), shape((1, COLS), f32),
         shape((PAST + CHIP_ROWS, DH), bf16), shape((CHIP_ROWS, COLS), f32), shape((1, COLS), f32),
         shape((1, COLS), f32)],
    )(query_rows, saved_out, out_grad, doc_lengths.reshape(1, 64), own)
    keys = call(keys_kernel, [shape((PAST, 2 * DH), bf16)], flops=3 * 10**9)(*fetched, bias)[0]
    q3, g3, far_dot = (swap_cores(x) for x in (q2, g2, row_dot))
    weights, tops, stats = call(
        score_kernel, [shape((PAST, columns), f32), shape((2, columns), f32), shape((4, COLS), f32)]
    )(q2, q3, keys, own_top, own_sum)
    far_stats = swap_cores(stats)
    slopes = call(slope_kernel, [shape((PAST, columns), f32)])(
        g2, g3, row_dot, far_dot, *fetched
    )[0]
    far_stats, slopes = together((far_stats, slopes))
    part_a, part_b, ds, norm = call(
        main_kernel,
        [shape((CHIP_ROWS, 2 * DH), bf16), shape((CHIP_ROWS, 2 * DH), bf16),
         shape((PAST, columns), bf16), shape((2, columns), f32)],
        [pltpu.VMEM((PAST, columns), bf16)],
    )(q2, q3, g2, g3, weights, slopes, tops, stats, far_stats)
    back = [move_chips(part, number, False) for number, part in enumerate((part_a, part_b))]
    query_grad, own_sums, *pieces = call(
        finish_kernel,
        [shape((COLS, DH), f32), shape((CHIP_ROWS, 2 * DH), f32)]
        + [shape((high - low, DH), bf16) for low, high in zip(PIECES, PIECES[1:])],
        [pltpu.VMEM((CHIP_ROWS, COLS), bf16)] * 2,
    )(q2, g2, row_dot, own_weights, own_top, norm, ds, own, *fetched)
    pieces = [swap_cores(piece) for piece in pieces]
    totals = back[1].astype(f32) + back[0].astype(f32) + own_sums
    far_totals = swap_cores(totals[ROWS:].astype(bf16))
    totals, query_grad = together((totals, query_grad))
    query_grad = call(add_kernel, [shape((ROWS, HQ * DH), bf16)])(query_grad, *pieces)[0]
    far_totals, query_grad = together((far_totals, query_grad))
    result = totals[:ROWS] + far_totals.astype(f32)
    result = result.astype(bf16)
    return (query_grad, result[:, :DH], result[:, DH:])


def solution(mesh):
    placed = P(AXES, None)
    return jax.shard_map(
        on_device,
        mesh=mesh,
        in_specs=(placed,) * 5 + (P(),),
        out_specs=(placed,) * 3,
        check_vma=False,
    )
```

```python
import functools
import math

import jax
import jax.numpy as jnp
from jax import lax
from jax.experimental import pallas as pl
from jax.experimental.pallas import tpu as pltpu
from jax.sharding import PartitionSpec as P

DH = 128
HQ = 16
ROWS = 64
CHUNKS = 256
CHIPS = CHUNKS // 2
HALF_CHUNKS = 8
HALVES = CHUNKS // HALF_CHUNKS
COLS = HQ * ROWS
CHIP_ROWS = 2 * ROWS
PAST = 2 * CHIP_ROWS
TILE = 256
TILES = COLS // TILE
NEG = -1e30
SCALING = 1.0 / math.sqrt(DH)
EXP2_SCALING = SCALING * math.log2(math.e)
AXES = ("blk", "uly")
MOVES = (
    ((1, 4), (0, 0, 0, 1), (1, 0, 0, 0)),
    ((3, 2), (0, 1, 0, 0), (0, 0, 1, 0)),
)
PIECES = (0, 352, 704, COLS)
KEY_COLS, VALUE_COLS = slice(0, DH), slice(DH, 2 * DH)


def device_of(chunk):
    half, place = divmod(chunk, HALF_CHUNKS)
    if half < HALVES // 2:
        return half * 16 + place
    return (HALVES - 1 - half) * 16 + 8 + place


def swap_cores(x):
    return lax.ppermute(x, "uly", [(i, i ^ 1) for i in range(16)])


def move_chips(x, number, forward):
    steps, sends, takes = MOVES[number]
    pairs = []
    for chip in range(CHIPS):
        for other, step in enumerate(steps):
            target = (chip + step) % CHIPS
            source = 2 * chip + (sends[chip % 4] ^ other)
            pair = (device_of(source), device_of(2 * target + (takes[target % 4] ^ other)))
            pairs.append(pair if forward else pair[::-1])
    return lax.ppermute(x, AXES, pairs)


def entry(table, index):
    value = table[3]
    for i in range(3):
        value = jnp.where(index == i, table[i], value)
    return value


def dot(a, b, contract):
    return lax.dot_general(a, b, (contract, ((), ())), preferred_element_type=jnp.float32)


def dot_nt(a, b):
    return dot(a, b, ((1,), (1,)))


def dot_nn(a, b):
    return dot(a, b, ((1,), (0,)))


def dot_tn(a, b):
    return dot(a, b, ((0,), (0,)))


def pack_kernel(mine_ref, other_k_ref, other_v_ref, w_ref):
    w_ref[:ROWS, :] = mine_ref[...]
    w_ref[ROWS:, :DH] = other_k_ref[...]
    w_ref[ROWS:, DH:] = other_v_ref[...]


def folded(x, op):
    return op(x.reshape(x.shape[0] // 8, 8, x.shape[1]), axis=0)


def tiles():
    for tile in range(2 * TILES):
        side, at = divmod(tile, TILES)
        yield slice(tile * TILE, (tile + 1) * TILE), side, slice(at * TILE, (at + 1) * TILE)


def query_tile(queries, side):
    row = lax.rem(lax.broadcasted_iota(jnp.int32, (DH, DH), 0), ROWS) + side * ROWS
    lane = lax.broadcasted_iota(jnp.int32, (DH, DH), 1)
    hot = (row == lane).astype(jnp.bfloat16)
    return jnp.concatenate([queries, jnp.concatenate([hot] * (queries.shape[0] // DH), axis=0)], axis=1)


def scored(scores):
    top = jnp.max(folded(scores, jnp.max), axis=0, keepdims=True)
    weights = jnp.exp2((scores - top) * EXP2_SCALING)
    return weights, top, jnp.sum(folded(weights, jnp.sum), axis=0, keepdims=True)


def layout_kernel(q_ref, q2_ref):
    for h in range(HQ):
        q2_ref[h * ROWS : (h + 1) * ROWS, :] = q_ref[:, h * DH : (h + 1) * DH]


def prepare_kernel(q2_ref, o_ref, g_ref, len_ref, own_ref,
                   g2_ref, dot_ref, bias_ref, e_ref, top_ref, sum_ref):
    blk = lax.axis_index("blk")
    uly = lax.axis_index("uly")
    core = lax.rem(uly, 2)
    place = lax.rem(uly, HALF_CHUNKS)
    half = jnp.where(uly < HALF_CHUNKS, blk, HALVES - 1 - blk)
    chunk = half * HALF_CHUNKS + place
    chip = chunk // 2

    ones = jnp.ones((8, DH), jnp.bfloat16)
    for h in range(HQ):
        cols = slice(h * DH, (h + 1) * DH)
        rows = slice(h * ROWS, (h + 1) * ROWS)
        grad = g_ref[:, cols]
        g2_ref[rows, :] = grad
        prod = grad.astype(jnp.float32) * o_ref[:, cols].astype(jnp.float32)
        high = prod.astype(jnp.bfloat16)
        low = (prod - high.astype(jnp.float32)).astype(jnp.bfloat16)
        dot_ref[:, rows] = (dot_nt(ones, high) + dot_nt(ones, low))[0:1]

    lens = jnp.broadcast_to(len_ref[...].astype(jnp.float32), (64, 64))
    doc = lax.broadcasted_iota(jnp.int32, (64, 64), 0)
    other = lax.broadcasted_iota(jnp.int32, (64, 64), 1)
    starts = jnp.sum(jnp.where(other < doc, lens, 0.0), axis=1, keepdims=True).astype(jnp.int32)
    lane = lax.broadcasted_iota(jnp.int32, (1, DH), 1)
    here = jnp.where(lane < ROWS, chunk, 2 * chip + 1 - core) * ROWS + lax.rem(lane, ROWS)
    first = jnp.max(jnp.where(starts <= here, starts, 0), axis=0, keepdims=True)
    index = lax.broadcasted_iota(jnp.int32, (ROWS, DH), 0)
    chunks = []
    place = lax.rem(chip, 4)
    for (first_step, second_step), sends, takes in MOVES:
        is_first = core == entry(takes, place)
        source = jnp.where(
            is_first,
            entry([sends[(y - first_step) % 4] for y in range(4)], place),
            entry([1 - sends[(y - second_step) % 4] for y in range(4)], place),
        )
        past = 2 * (chip - jnp.where(is_first, first_step, second_step))
        chunks += [past + source, past + 1 - source]
    for part, key_chunk in enumerate(chunks + [chunk, 2 * chip + 1 - core]):
        where = key_chunk * ROWS + index
        bias = jnp.where((where >= first) & (where <= here), 0.0, NEG).astype(jnp.bfloat16)
        bias_ref[part * ROWS : (part + 1) * ROWS, :] = bias
    keys = jnp.concatenate([own_ref[:, KEY_COLS], bias_ref[PAST:, :]], axis=1)
    for tile in range(TILES):
        cols = slice(tile * TILE, (tile + 1) * TILE)
        e_ref[:, cols], top_ref[:, cols], sum_ref[:, cols] = scored(
            dot_nt(keys, query_tile(q2_ref[cols, :], 0))
        )


def keys_kernel(a_ref, b_ref, bias_ref, keys_ref):
    for ref, group in zip((a_ref, b_ref), GROUPS):
        keys_ref[group, :DH] = ref[:, KEY_COLS]
    keys_ref[:, DH:] = bias_ref[:PAST, :]


GROUPS = (slice(0, CHIP_ROWS), slice(CHIP_ROWS, PAST))


def score_kernel(q_ref, partner_q_ref, keys_ref, own_top_ref, own_sum_ref,
                 e_ref, tops_ref, stats_ref):
    for side, ref in enumerate((q_ref, partner_q_ref)):
        e_ref[:, side * COLS : (side + 1) * COLS] = dot_nt(keys_ref[...], query_tile(ref[...], side))
    for at in range(0, 2 * COLS, DH):
        side, start = divmod(at, COLS)
        cols, rows = slice(at, at + DH), slice(start, start + DH)
        tops, sums = [], []
        for i, group in enumerate(GROUPS):
            e_ref[group, cols], top, total = scored(e_ref[group, cols])
            tops_ref[i : i + 1, cols] = top
            tops.append(top)
            sums.append(total)
        if side == 0:
            tops.append(own_top_ref[:, rows])
            sums.append(own_sum_ref[:, rows])
        most = functools.reduce(jnp.maximum, tops)
        stats_ref[2 * side : 2 * side + 1, rows] = most
        stats_ref[2 * side + 1 : 2 * side + 2, rows] = sum(
            x * jnp.exp2((top - most) * EXP2_SCALING) for x, top in zip(sums, tops)
        )


def slope_kernel(g_ref, partner_g_ref, dot_ref, partner_dot_ref, a_ref, b_ref, u_ref):
    values = jnp.concatenate([a_ref[:, VALUE_COLS], b_ref[:, VALUE_COLS]], axis=0)
    for cols, side, rows in tiles():
        grad = (g_ref, partner_g_ref)[side][rows, :]
        u_ref[:, cols] = dot_nt(values, grad) - (dot_ref, partner_dot_ref)[side][:, rows]


def dot_sides(left_ref, own_ref, partner_ref):
    return dot_nn(left_ref[:, :COLS], own_ref[...]) + dot_nn(left_ref[:, COLS:], partner_ref[...])


def main_kernel(q_ref, partner_q_ref, g_ref, partner_g_ref, e_ref, u_ref, tops_ref, stats_ref, far_ref,
                a_ref, b_ref, ds_ref, norm_ref, p_ref):
    for side in range(2):
        near, far = 2 * side, 2 - 2 * side
        top, far_top = stats_ref[near : near + 1, :], far_ref[far : far + 1, :]
        most = jnp.maximum(top, far_top)
        total = stats_ref[near + 1 : near + 2, :] * jnp.exp2(
            (top - most) * EXP2_SCALING
        ) + far_ref[far + 1 : far + 2, :] * jnp.exp2((far_top - most) * EXP2_SCALING)
        columns = slice(side * COLS, (side + 1) * COLS)
        norm_ref[0:1, columns] = most
        norm_ref[1:2, columns] = total
        factors = jnp.exp2((tops_ref[:, columns] - most) * EXP2_SCALING) * (1.0 / total)
        for start in range(0, COLS, TILE):
            cols = slice(side * COLS + start, side * COLS + start + TILE)
            for i, group in enumerate(GROUPS):
                weights = e_ref[group, cols] * factors[i : i + 1, start : start + TILE]
                ds_ref[group, cols] = (weights * u_ref[group, cols]).astype(jnp.bfloat16)
                p_ref[group, cols] = weights.astype(jnp.bfloat16)
    key_grads = (dot_sides(ds_ref, q_ref, partner_q_ref) * SCALING).astype(jnp.bfloat16)
    value_grads = dot_sides(p_ref, g_ref, partner_g_ref).astype(jnp.bfloat16)
    for ref, group in zip((a_ref, b_ref), GROUPS):
        ref[:, KEY_COLS] = key_grads[group]
        ref[:, VALUE_COLS] = value_grads[group]


def finish_kernel(q_ref, g_ref, dot_ref, own_e_ref, own_top_ref, norm_ref, ds_ref, own_ref, a_ref, b_ref,
                  dq_ref, own_sum_ref, *rest):
    *piece_refs, own_p_ref, own_ds_ref = rest
    past_keys = jnp.concatenate([a_ref[:, KEY_COLS], b_ref[:, KEY_COLS]], axis=0)
    for cols, side, rows in reversed(list(tiles())):
        grads = dot_tn(past_keys, ds_ref[:, cols])
        if side == 0:
            slopes = dot_nt(own_ref[:, VALUE_COLS], g_ref[rows, :]) - dot_ref[:, rows]
            factor = jnp.exp2((own_top_ref[:, rows] - norm_ref[0:1, rows]) * EXP2_SCALING)
            weights = own_e_ref[:, rows] * (factor / norm_ref[1:2, rows])
            own_ds = (weights * slopes).astype(jnp.bfloat16)
            own_p_ref[:, rows] = weights.astype(jnp.bfloat16)
            own_ds_ref[:, rows] = own_ds
            grads = grads + dot_tn(own_ref[:, KEY_COLS], own_ds)
        grads = grads * SCALING
        for j in range(TILE // DH):
            pair = grads[:, j * DH : (j + 1) * DH].T
            at = rows.start + j * DH
            if side == 0:
                dq_ref[at : at + DH, :] = pair
                continue
            for start, ref in zip(PIECES, piece_refs):
                low, high = max(at, start), min(at + DH, start + ref.shape[0])
                if low < high:
                    ref[low - start : high - start, :] = pair[low - at : high - at].astype(jnp.bfloat16)
    own_sum_ref[:, KEY_COLS] = dot_nn(own_ds_ref[...], q_ref[...]) * SCALING
    own_sum_ref[:, VALUE_COLS] = dot_nn(own_p_ref[...], g_ref[...])


def add_kernel(dq_ref, *refs):
    *piece_refs, sum_ref = refs
    for h in range(HQ):
        total = dq_ref[h * ROWS : (h + 1) * ROWS, :]
        low = h * ROWS
        parts = []
        for start, ref in zip(PIECES, piece_refs):
            first, last = max(low, start), min(low + ROWS, start + ref.shape[0])
            if first < last:
                parts.append(ref[first - start : last - start, :].astype(jnp.float32))
        partner = parts[0] if len(parts) == 1 else jnp.concatenate(parts, axis=0)
        sum_ref[:, h * DH : (h + 1) * DH] = (total + partner).astype(jnp.bfloat16)


def call(kernel, outs, scratch=(), flops=10**9):
    vmem = pl.BlockSpec(memory_space=pltpu.VMEM)
    return lambda *args: pl.pallas_call(
        kernel,
        out_shape=outs,
        in_specs=[vmem] * len(args),
        out_specs=[vmem] * len(outs),
        scratch_shapes=list(scratch),
        compiler_params=pltpu.CompilerParams(vmem_limit_bytes=24 * 1024 * 1024),
        cost_estimate=pl.CostEstimate(flops=flops, bytes_accessed=flops // 500, transcendentals=0),
    )(*args)


def on_device(query_rows, key_rows, value_rows, saved_out, out_grad, doc_lengths):
    shape = jax.ShapeDtypeStruct
    bf16, f32 = jnp.bfloat16, jnp.float32
    together = lax.optimization_barrier
    other = (swap_cores(key_rows), swap_cores(value_rows))
    mine = jnp.concatenate([key_rows, value_rows], axis=1)
    other, mine = together((other, mine))
    own = call(pack_kernel, [shape((CHIP_ROWS, 2 * DH), bf16)])(mine, *other)[0]
    fetched = [move_chips(own, number, True) for number in range(2)]
    columns = 2 * COLS
    q2 = call(layout_kernel, [shape((COLS, DH), bf16)], flops=10**8)(query_rows)[0]
    g2, row_dot, bias, own_weights, own_top, own_sum = call(
        prepare_kernel,
        [shape((COLS, DH), bf16), shape((1, COLS), f32),
         shape((PAST + CHIP_ROWS, DH), bf16), shape((CHIP_ROWS, COLS), f32), shape((1, COLS), f32),
         shape((1, COLS), f32)],
        flops=10**8,
    )(q2, saved_out, out_grad, doc_lengths.reshape(1, 64), own)
    keys = call(keys_kernel, [shape((PAST, 2 * DH), bf16)], flops=4 * 10**9)(*fetched, bias)[0]
    q3, g3, far_dot = (swap_cores(x) for x in (q2, g2, row_dot))
    weights, tops, stats = call(
        score_kernel, [shape((PAST, columns), f32), shape((2, columns), f32), shape((4, COLS), f32)]
    )(q2, q3, keys, own_top, own_sum)
    far_stats = swap_cores(stats)
    slopes = call(slope_kernel, [shape((PAST, columns), f32)])(
        g2, g3, row_dot, far_dot, *fetched
    )[0]
    far_stats, slopes = together((far_stats, slopes))
    part_a, part_b, ds, norm = call(
        main_kernel,
        [shape((CHIP_ROWS, 2 * DH), bf16), shape((CHIP_ROWS, 2 * DH), bf16),
         shape((PAST, columns), bf16), shape((2, columns), f32)],
        [pltpu.VMEM((PAST, columns), bf16)],
    )(q2, q3, g2, g3, weights, slopes, tops, stats, far_stats)
    back = [move_chips(part, number, False) for number, part in enumerate((part_a, part_b))]
    query_grad, own_sums, *pieces = call(
        finish_kernel,
        [shape((COLS, DH), f32), shape((CHIP_ROWS, 2 * DH), f32)]
        + [shape((high - low, DH), bf16) for low, high in zip(PIECES, PIECES[1:])],
        [pltpu.VMEM((CHIP_ROWS, COLS), bf16)] * 2,
    )(q2, g2, row_dot, own_weights, own_top, norm, ds, own, *fetched)
    pieces = [swap_cores(piece) for piece in pieces]
    totals = back[1].astype(f32) + back[0].astype(f32) + own_sums
    far_totals = swap_cores(totals[ROWS:].astype(bf16))
    totals, query_grad = together((totals, query_grad))
    query_grad = call(add_kernel, [shape((ROWS, HQ * DH), bf16)])(query_grad, *pieces)[0]
    far_totals, query_grad = together((far_totals, query_grad))
    result = totals[:ROWS] + far_totals.astype(f32)
    result = result.astype(bf16)
    return (query_grad, result[:, :DH], result[:, DH:])


def solution(mesh):
    placed = P(AXES, None)
    return jax.shard_map(
        on_device,
        mesh=mesh,
        in_specs=(placed,) * 5 + (P(),),
        out_specs=(placed,) * 3,
        check_vma=False,
    )
```

```python
import functools
import math

import jax
import jax.numpy as jnp
from jax import lax
from jax.experimental import pallas as pl
from jax.experimental.pallas import tpu as pltpu
from jax.sharding import PartitionSpec as P

DH = 128
HQ = 16
ROWS = 64
CHUNKS = 256
CHIPS = CHUNKS // 2
HALF_CHUNKS = 8
HALVES = CHUNKS // HALF_CHUNKS
COLS = HQ * ROWS
CHIP_ROWS = 2 * ROWS
PAST = 2 * CHIP_ROWS
TILE = 256
TILES = COLS // TILE
NEG = -1e30
SCALING = 1.0 / math.sqrt(DH)
EXP2_SCALING = SCALING * math.log2(math.e)
AXES = ("blk", "uly")
MOVES = (
    ((1, 4), (0, 0, 0, 1), (1, 0, 0, 0)),
    ((3, 2), (0, 1, 0, 0), (0, 0, 1, 0)),
)
PIECES = (0, 352, 704, COLS)
KEY_COLS, VALUE_COLS = slice(0, DH), slice(DH, 2 * DH)


def device_of(chunk):
    half, place = divmod(chunk, HALF_CHUNKS)
    if half < HALVES // 2:
        return half * 16 + place
    return (HALVES - 1 - half) * 16 + 8 + place


def swap_cores(x):
    return lax.ppermute(x, "uly", [(i, i ^ 1) for i in range(16)])


def move_chips(x, number, forward):
    steps, sends, takes = MOVES[number]
    pairs = []
    for chip in range(CHIPS):
        for other, step in enumerate(steps):
            target = (chip + step) % CHIPS
            source = 2 * chip + (sends[chip % 4] ^ other)
            pair = (device_of(source), device_of(2 * target + (takes[target % 4] ^ other)))
            pairs.append(pair if forward else pair[::-1])
    return lax.ppermute(x, AXES, pairs)


def entry(table, index):
    value = table[3]
    for i in range(3):
        value = jnp.where(index == i, table[i], value)
    return value


def dot(a, b, contract):
    return lax.dot_general(a, b, (contract, ((), ())), preferred_element_type=jnp.float32)


def dot_nt(a, b):
    return dot(a, b, ((1,), (1,)))


def dot_nn(a, b):
    return dot(a, b, ((1,), (0,)))


def dot_tn(a, b):
    return dot(a, b, ((0,), (0,)))


def pack_kernel(mine_ref, other_k_ref, other_v_ref, w_ref):
    w_ref[:ROWS, :] = mine_ref[...]
    w_ref[ROWS:, :DH] = other_k_ref[...]
    w_ref[ROWS:, DH:] = other_v_ref[...]


def folded(x, op):
    return op(x.reshape(x.shape[0] // 8, 8, x.shape[1]), axis=0)


def tiles():
    for tile in range(2 * TILES):
        side, at = divmod(tile, TILES)
        yield slice(tile * TILE, (tile + 1) * TILE), side, slice(at * TILE, (at + 1) * TILE)


def query_tile(queries, side):
    row = lax.rem(lax.broadcasted_iota(jnp.int32, (DH, DH), 0), ROWS) + side * ROWS
    lane = lax.broadcasted_iota(jnp.int32, (DH, DH), 1)
    hot = (row == lane).astype(jnp.bfloat16)
    return jnp.concatenate([queries, jnp.concatenate([hot] * (queries.shape[0] // DH), axis=0)], axis=1)


def scored(scores):
    top = jnp.max(folded(scores, jnp.max), axis=0, keepdims=True)
    weights = jnp.exp2((scores - top) * EXP2_SCALING)
    return weights, top, jnp.sum(folded(weights, jnp.sum), axis=0, keepdims=True)


def layout_kernel(q_ref, q2_ref):
    for h in range(HQ):
        q2_ref[h * ROWS : (h + 1) * ROWS, :] = q_ref[:, h * DH : (h + 1) * DH]


def prepare_kernel(q2_ref, o_ref, g_ref, len_ref, own_ref,
                   g2_ref, dot_ref, bias_ref, e_ref, top_ref, sum_ref):
    blk = lax.axis_index("blk")
    uly = lax.axis_index("uly")
    core = lax.rem(uly, 2)
    place = lax.rem(uly, HALF_CHUNKS)
    half = jnp.where(uly < HALF_CHUNKS, blk, HALVES - 1 - blk)
    chunk = half * HALF_CHUNKS + place
    chip = chunk // 2

    ones = jnp.ones((8, DH), jnp.bfloat16)
    for h in range(HQ):
        cols = slice(h * DH, (h + 1) * DH)
        rows = slice(h * ROWS, (h + 1) * ROWS)
        grad = g_ref[:, cols]
        g2_ref[rows, :] = grad
        prod = grad.astype(jnp.float32) * o_ref[:, cols].astype(jnp.float32)
        high = prod.astype(jnp.bfloat16)
        low = (prod - high.astype(jnp.float32)).astype(jnp.bfloat16)
        dot_ref[:, rows] = (dot_nt(ones, high) + dot_nt(ones, low))[0:1]

    lens = jnp.broadcast_to(len_ref[...].astype(jnp.float32), (64, 64))
    doc = lax.broadcasted_iota(jnp.int32, (64, 64), 0)
    other = lax.broadcasted_iota(jnp.int32, (64, 64), 1)
    starts = jnp.sum(jnp.where(other < doc, lens, 0.0), axis=1, keepdims=True).astype(jnp.int32)
    lane = lax.broadcasted_iota(jnp.int32, (1, DH), 1)
    here = jnp.where(lane < ROWS, chunk, 2 * chip + 1 - core) * ROWS + lax.rem(lane, ROWS)
    first = jnp.max(jnp.where(starts <= here, starts, 0), axis=0, keepdims=True)
    index = lax.broadcasted_iota(jnp.int32, (ROWS, DH), 0)
    chunks = []
    place = lax.rem(chip, 4)
    for (first_step, second_step), sends, takes in MOVES:
        is_first = core == entry(takes, place)
        source = jnp.where(
            is_first,
            entry([sends[(y - first_step) % 4] for y in range(4)], place),
            entry([1 - sends[(y - second_step) % 4] for y in range(4)], place),
        )
        past = 2 * (chip - jnp.where(is_first, first_step, second_step))
        chunks += [past + source, past + 1 - source]
    for part, key_chunk in enumerate(chunks + [chunk, 2 * chip + 1 - core]):
        where = key_chunk * ROWS + index
        bias = jnp.where((where >= first) & (where <= here), 0.0, NEG).astype(jnp.bfloat16)
        bias_ref[part * ROWS : (part + 1) * ROWS, :] = bias
    keys = jnp.concatenate([own_ref[:, KEY_COLS], bias_ref[PAST:, :]], axis=1)
    for tile in range(TILES):
        cols = slice(tile * TILE, (tile + 1) * TILE)
        e_ref[:, cols], top_ref[:, cols], sum_ref[:, cols] = scored(
            dot_nt(keys, query_tile(q2_ref[cols, :], 0))
        )


def keys_kernel(a_ref, b_ref, bias_ref, keys_ref):
    for ref, group in zip((a_ref, b_ref), GROUPS):
        keys_ref[group, :DH] = ref[:, KEY_COLS]
    keys_ref[:, DH:] = bias_ref[:PAST, :]


GROUPS = (slice(0, CHIP_ROWS), slice(CHIP_ROWS, PAST))


def score_kernel(q_ref, partner_q_ref, keys_ref, own_top_ref, own_sum_ref, dot_ref,
                 e_ref, tops_ref, stats_ref):
    stats_ref[4:5, :] = dot_ref[...]
    for side, ref in enumerate((q_ref, partner_q_ref)):
        e_ref[:, side * COLS : (side + 1) * COLS] = dot_nt(keys_ref[...], query_tile(ref[...], side))
    for at in range(0, 2 * COLS, DH):
        side, start = divmod(at, COLS)
        cols, rows = slice(at, at + DH), slice(start, start + DH)
        tops, sums = [], []
        for i, group in enumerate(GROUPS):
            e_ref[group, cols], top, total = scored(e_ref[group, cols])
            tops_ref[i : i + 1, cols] = top
            tops.append(top)
            sums.append(total)
        if side == 0:
            tops.append(own_top_ref[:, rows])
            sums.append(own_sum_ref[:, rows])
        most = functools.reduce(jnp.maximum, tops)
        stats_ref[2 * side : 2 * side + 1, rows] = most
        stats_ref[2 * side + 1 : 2 * side + 2, rows] = sum(
            x * jnp.exp2((top - most) * EXP2_SCALING) for x, top in zip(sums, tops)
        )


def slope_kernel(g_ref, partner_g_ref, a_ref, b_ref, u_ref):
    values = jnp.concatenate([a_ref[:, VALUE_COLS], b_ref[:, VALUE_COLS]], axis=0)
    for cols, side, rows in tiles():
        u_ref[:, cols] = dot_nt(values, (g_ref, partner_g_ref)[side][rows, :])


def dot_sides(left_ref, own_ref, partner_ref):
    return dot_nn(left_ref[:, :COLS], own_ref[...]) + dot_nn(left_ref[:, COLS:], partner_ref[...])


def weigh(e_ref, u_ref, factors, row_dots, side, group, ds_ref, p_ref):
    for start in range(0, COLS, TILE):
        cols = slice(side * COLS + start, side * COLS + start + TILE)
        weights = e_ref[group, cols] * factors[:, start : start + TILE]
        slopes = u_ref[group, cols] - row_dots[:, start : start + TILE]
        ds_ref[:, cols] = (weights * slopes).astype(jnp.bfloat16)
        p_ref[:, cols] = weights.astype(jnp.bfloat16)


def key_sums(q_ref, partner_q_ref, g_ref, partner_g_ref, ds_ref, p_ref, part_ref):
    part_ref[:, KEY_COLS] = (dot_sides(ds_ref, q_ref, partner_q_ref) * SCALING).astype(jnp.bfloat16)
    part_ref[:, VALUE_COLS] = dot_sides(p_ref, g_ref, partner_g_ref).astype(jnp.bfloat16)


def main_kernel(q_ref, partner_q_ref, g_ref, partner_g_ref, e_ref, u_ref, tops_ref, stats_ref, far_ref,
                part_ref, ds_ref, norm_ref, factors_ref, p_ref):
    for side in range(2):
        near, far = 2 * side, 2 - 2 * side
        top, far_top = stats_ref[near : near + 1, :], far_ref[far : far + 1, :]
        most = jnp.maximum(top, far_top)
        total = stats_ref[near + 1 : near + 2, :] * jnp.exp2(
            (top - most) * EXP2_SCALING
        ) + far_ref[far + 1 : far + 2, :] * jnp.exp2((far_top - most) * EXP2_SCALING)
        columns = slice(side * COLS, (side + 1) * COLS)
        norm_ref[0:1, columns] = most
        norm_ref[1:2, columns] = total
        factors = jnp.exp2((tops_ref[:, columns] - most) * EXP2_SCALING) * (1.0 / total)
        row_dots = (stats_ref, far_ref)[side][4:5, :]
        factors_ref[0:1, columns] = factors[0:1]
        factors_ref[1:2, columns] = row_dots
        weigh(e_ref, u_ref, factors[1:2], row_dots, side, GROUPS[1], ds_ref, p_ref)
    key_sums(q_ref, partner_q_ref, g_ref, partner_g_ref, ds_ref, p_ref, part_ref)


def rest_kernel(q_ref, partner_q_ref, g_ref, partner_g_ref, e_ref, u_ref, factors_ref,
                part_ref, ds_ref, p_ref):
    for side in range(2):
        factors = factors_ref[:, side * COLS : (side + 1) * COLS]
        weigh(e_ref, u_ref, factors[0:1], factors[1:2], side, GROUPS[0], ds_ref, p_ref)
    key_sums(q_ref, partner_q_ref, g_ref, partner_g_ref, ds_ref, p_ref, part_ref)


def total_kernel(back_ref, own_ref, total_ref):
    total_ref[...] = back_ref[...].astype(jnp.float32) + own_ref[...]


def finish_kernel(q_ref, g_ref, dot_ref, own_e_ref, own_top_ref, norm_ref, near_ds_ref, ds_ref, own_ref, a_ref, b_ref,
                  dq_ref, own_sum_ref, *rest):
    *piece_refs, own_p_ref, own_ds_ref = rest
    past_keys = jnp.concatenate([a_ref[:, KEY_COLS], b_ref[:, KEY_COLS]], axis=0)
    for cols, side, rows in reversed(list(tiles())):
        ds = jnp.concatenate([near_ds_ref[:, cols], ds_ref[:, cols]], axis=0)
        grads = dot_tn(past_keys, ds)
        if side == 0:
            slopes = dot_nt(own_ref[:, VALUE_COLS], g_ref[rows, :]) - dot_ref[:, rows]
            factor = jnp.exp2((own_top_ref[:, rows] - norm_ref[0:1, rows]) * EXP2_SCALING)
            weights = own_e_ref[:, rows] * (factor / norm_ref[1:2, rows])
            own_ds = (weights * slopes).astype(jnp.bfloat16)
            own_p_ref[:, rows] = weights.astype(jnp.bfloat16)
            own_ds_ref[:, rows] = own_ds
            grads = grads + dot_tn(own_ref[:, KEY_COLS], own_ds)
        grads = grads * SCALING
        for j in range(TILE // DH):
            pair = grads[:, j * DH : (j + 1) * DH].T
            at = rows.start + j * DH
            if side == 0:
                dq_ref[at : at + DH, :] = pair
                continue
            for start, ref in zip(PIECES, piece_refs):
                low, high = max(at, start), min(at + DH, start + ref.shape[0])
                if low < high:
                    ref[low - start : high - start, :] = pair[low - at : high - at].astype(jnp.bfloat16)
    own_sum_ref[:, KEY_COLS] = dot_nn(own_ds_ref[...], q_ref[...]) * SCALING
    own_sum_ref[:, VALUE_COLS] = dot_nn(own_p_ref[...], g_ref[...])


def add_kernel(dq_ref, *refs):
    *piece_refs, sum_ref = refs
    for h in range(HQ):
        total = dq_ref[h * ROWS : (h + 1) * ROWS, :]
        low = h * ROWS
        parts = []
        for start, ref in zip(PIECES, piece_refs):
            first, last = max(low, start), min(low + ROWS, start + ref.shape[0])
            if first < last:
                parts.append(ref[first - start : last - start, :].astype(jnp.float32))
        partner = parts[0] if len(parts) == 1 else jnp.concatenate(parts, axis=0)
        sum_ref[:, h * DH : (h + 1) * DH] = (total + partner).astype(jnp.bfloat16)


def call(kernel, outs, scratch=(), flops=10**9):
    vmem = pl.BlockSpec(memory_space=pltpu.VMEM)
    return lambda *args: pl.pallas_call(
        kernel,
        out_shape=outs,
        in_specs=[vmem] * len(args),
        out_specs=[vmem] * len(outs),
        scratch_shapes=list(scratch),
        compiler_params=pltpu.CompilerParams(vmem_limit_bytes=24 * 1024 * 1024),
        cost_estimate=pl.CostEstimate(flops=flops, bytes_accessed=flops // 500, transcendentals=0),
    )(*args)


def on_device(query_rows, key_rows, value_rows, saved_out, out_grad, doc_lengths):
    shape = jax.ShapeDtypeStruct
    bf16, f32 = jnp.bfloat16, jnp.float32
    together = lax.optimization_barrier
    other = (swap_cores(key_rows), swap_cores(value_rows))
    mine = jnp.concatenate([key_rows, value_rows], axis=1)
    other, mine = together((other, mine))
    own = call(pack_kernel, [shape((CHIP_ROWS, 2 * DH), bf16)])(mine, *other)[0]
    fetched = [move_chips(own, number, True) for number in range(2)]
    columns = 2 * COLS
    q2 = call(layout_kernel, [shape((COLS, DH), bf16)], flops=10**8)(query_rows)[0]
    g2, row_dot, bias, own_weights, own_top, own_sum = call(
        prepare_kernel,
        [shape((COLS, DH), bf16), shape((1, COLS), f32),
         shape((PAST + CHIP_ROWS, DH), bf16), shape((CHIP_ROWS, COLS), f32), shape((1, COLS), f32),
         shape((1, COLS), f32)],
        flops=10**8,
    )(q2, saved_out, out_grad, doc_lengths.reshape(1, 64), own)
    keys = call(keys_kernel, [shape((PAST, 2 * DH), bf16)], flops=4 * 10**9)(*fetched, bias)[0]
    q3, g3 = swap_cores(q2), swap_cores(g2)
    weights, tops, stats = call(
        score_kernel, [shape((PAST, columns), f32), shape((2, columns), f32), shape((5, COLS), f32)]
    )(q2, q3, keys, own_top, own_sum, row_dot)
    far_stats = swap_cores(stats)
    slopes = call(slope_kernel, [shape((PAST, columns), f32)])(g2, g3, *fetched)[0]
    far_stats, slopes = together((far_stats, slopes))
    part_b, ds, norm, factors = call(
        main_kernel,
        [shape((CHIP_ROWS, 2 * DH), bf16), shape((CHIP_ROWS, columns), bf16), shape((2, columns), f32),
         shape((2, columns), f32)],
        [pltpu.VMEM((CHIP_ROWS, columns), bf16)],
    )(q2, q3, g2, g3, weights, slopes, tops, stats, far_stats)
    part_a, near_ds = call(
        rest_kernel,
        [shape((CHIP_ROWS, 2 * DH), bf16), shape((CHIP_ROWS, columns), bf16)],
        [pltpu.VMEM((CHIP_ROWS, columns), bf16)],
    )(q2, q3, g2, g3, weights, slopes, factors)
    back = [move_chips(part, number, False) for number, part in enumerate((part_a, part_b))]
    query_grad, own_sums, *pieces = call(
        finish_kernel,
        [shape((COLS, DH), f32), shape((CHIP_ROWS, 2 * DH), f32)]
        + [shape((high - low, DH), bf16) for low, high in zip(PIECES, PIECES[1:])],
        [pltpu.VMEM((CHIP_ROWS, COLS), bf16)] * 2,
        flops=10**8,
    )(q2, g2, row_dot, own_weights, own_top, norm, near_ds, ds, own, *fetched)
    pieces = [swap_cores(piece) for piece in pieces]
    totals = call(total_kernel, [shape((CHIP_ROWS, 2 * DH), f32)], flops=5 * 10**9)(back[1], own_sums)[0]
    totals = totals + back[0].astype(f32)
    far_totals = swap_cores(totals[ROWS:].astype(bf16))
    totals, query_grad = together((totals, query_grad))
    query_grad = call(add_kernel, [shape((ROWS, HQ * DH), bf16)])(query_grad, *pieces)[0]
    far_totals, query_grad = together((far_totals, query_grad))
    result = totals[:ROWS] + far_totals.astype(f32)
    result = result.astype(bf16)
    return (query_grad, result[:, :DH], result[:, DH:])


def solution(mesh):
    placed = P(AXES, None)
    return jax.shard_map(
        on_device,
        mesh=mesh,
        in_specs=(placed,) * 5 + (P(),),
        out_specs=(placed,) * 3,
        check_vma=False,
    )
```

```python
import functools
import math

import jax
import jax.numpy as jnp
from jax import lax
from jax.experimental import pallas as pl
from jax.experimental.pallas import tpu as pltpu
from jax.sharding import PartitionSpec as P

DH = 128
HQ = 16
ROWS = 64
CHUNKS = 256
CHIPS = CHUNKS // 2
HALF_CHUNKS = 8
HALVES = CHUNKS // HALF_CHUNKS
COLS = HQ * ROWS
CHIP_ROWS = 2 * ROWS
PAST = 2 * CHIP_ROWS
TILE = 1024
TILES = COLS // TILE
NEG = -1e30
SCALING = 1.0 / math.sqrt(DH)
EXP2_SCALING = SCALING * math.log2(math.e)
AXES = ("blk", "uly")
MOVES = (
    ((1, 4), (0, 0, 0, 1), (1, 0, 0, 0)),
    ((3, 2), (0, 1, 0, 0), (0, 0, 1, 0)),
)
PIECES = (0, 352, 704, COLS)
KEY_COLS, VALUE_COLS = slice(0, DH), slice(DH, 2 * DH)


def device_of(chunk):
    half, place = divmod(chunk, HALF_CHUNKS)
    if half < HALVES // 2:
        return half * 16 + place
    return (HALVES - 1 - half) * 16 + 8 + place


def swap_cores(x):
    return lax.ppermute(x, "uly", [(i, i ^ 1) for i in range(16)])


def move_chips(x, number, forward):
    steps, sends, takes = MOVES[number]
    pairs = []
    for chip in range(CHIPS):
        for other, step in enumerate(steps):
            target = (chip + step) % CHIPS
            source = 2 * chip + (sends[chip % 4] ^ other)
            pair = (device_of(source), device_of(2 * target + (takes[target % 4] ^ other)))
            pairs.append(pair if forward else pair[::-1])
    return lax.ppermute(x, AXES, pairs)


def entry(table, index):
    value = table[3]
    for i in range(3):
        value = jnp.where(index == i, table[i], value)
    return value


def dot(a, b, contract):
    return lax.dot_general(a, b, (contract, ((), ())), preferred_element_type=jnp.float32)


def dot_nt(a, b):
    return dot(a, b, ((1,), (1,)))


def dot_nn(a, b):
    return dot(a, b, ((1,), (0,)))


def dot_tn(a, b):
    return dot(a, b, ((0,), (0,)))


def pack_kernel(mine_ref, other_k_ref, other_v_ref, w_ref):
    w_ref[:ROWS, :] = mine_ref[...]
    w_ref[ROWS:, :DH] = other_k_ref[...]
    w_ref[ROWS:, DH:] = other_v_ref[...]


def folded(x, op):
    return op(x.reshape(x.shape[0] // 8, 8, x.shape[1]), axis=0)


def tiles():
    for tile in range(2 * TILES):
        side, at = divmod(tile, TILES)
        yield slice(tile * TILE, (tile + 1) * TILE), side, slice(at * TILE, (at + 1) * TILE)


def query_tile(queries, side):
    row = lax.rem(lax.broadcasted_iota(jnp.int32, (DH, DH), 0), ROWS) + side * ROWS
    lane = lax.broadcasted_iota(jnp.int32, (DH, DH), 1)
    hot = (row == lane).astype(jnp.bfloat16)
    return jnp.concatenate([queries, jnp.concatenate([hot] * (queries.shape[0] // DH), axis=0)], axis=1)


def scored(scores):
    top = jnp.max(folded(scores, jnp.max), axis=0, keepdims=True)
    weights = jnp.exp2((scores - top) * EXP2_SCALING)
    return weights, top, jnp.sum(folded(weights, jnp.sum), axis=0, keepdims=True)


def layout_kernel(q_ref, q2_ref):
    for h in range(HQ):
        q2_ref[h * ROWS : (h + 1) * ROWS, :] = q_ref[:, h * DH : (h + 1) * DH]


def prepare_kernel(q2_ref, o_ref, g_ref, len_ref, own_ref,
                   g2_ref, dot_ref, bias_ref, e_ref, top_ref, sum_ref):
    blk = lax.axis_index("blk")
    uly = lax.axis_index("uly")
    core = lax.rem(uly, 2)
    place = lax.rem(uly, HALF_CHUNKS)
    half = jnp.where(uly < HALF_CHUNKS, blk, HALVES - 1 - blk)
    chunk = half * HALF_CHUNKS + place
    chip = chunk // 2

    ones = jnp.ones((8, DH), jnp.bfloat16)
    for h in range(HQ):
        cols = slice(h * DH, (h + 1) * DH)
        rows = slice(h * ROWS, (h + 1) * ROWS)
        grad = g_ref[:, cols]
        g2_ref[rows, :] = grad
        prod = grad.astype(jnp.float32) * o_ref[:, cols].astype(jnp.float32)
        high = prod.astype(jnp.bfloat16)
        low = (prod - high.astype(jnp.float32)).astype(jnp.bfloat16)
        dot_ref[:, rows] = (dot_nt(ones, high) + dot_nt(ones, low))[0:1]

    lens = jnp.broadcast_to(len_ref[...].astype(jnp.float32), (64, 64))
    doc = lax.broadcasted_iota(jnp.int32, (64, 64), 0)
    other = lax.broadcasted_iota(jnp.int32, (64, 64), 1)
    starts = jnp.sum(jnp.where(other < doc, lens, 0.0), axis=1, keepdims=True).astype(jnp.int32)
    lane = lax.broadcasted_iota(jnp.int32, (1, DH), 1)
    here = jnp.where(lane < ROWS, chunk, 2 * chip + 1 - core) * ROWS + lax.rem(lane, ROWS)
    first = jnp.max(jnp.where(starts <= here, starts, 0), axis=0, keepdims=True)
    index = lax.broadcasted_iota(jnp.int32, (ROWS, DH), 0)
    chunks = []
    place = lax.rem(chip, 4)
    for (first_step, second_step), sends, takes in MOVES:
        is_first = core == entry(takes, place)
        source = jnp.where(
            is_first,
            entry([sends[(y - first_step) % 4] for y in range(4)], place),
            entry([1 - sends[(y - second_step) % 4] for y in range(4)], place),
        )
        past = 2 * (chip - jnp.where(is_first, first_step, second_step))
        chunks += [past + source, past + 1 - source]
    for part, key_chunk in enumerate(chunks + [chunk, 2 * chip + 1 - core]):
        where = key_chunk * ROWS + index
        bias = jnp.where((where >= first) & (where <= here), 0.0, NEG).astype(jnp.bfloat16)
        bias_ref[part * ROWS : (part + 1) * ROWS, :] = bias
    keys = jnp.concatenate([own_ref[:, KEY_COLS], bias_ref[PAST:, :]], axis=1)
    for tile in range(TILES):
        cols = slice(tile * TILE, (tile + 1) * TILE)
        e_ref[:, cols], top_ref[:, cols], sum_ref[:, cols] = scored(
            dot_nt(keys, query_tile(q2_ref[cols, :], 0))
        )


def keys_kernel(a_ref, b_ref, bias_ref, keys_ref):
    for ref, group in zip((a_ref, b_ref), GROUPS):
        keys_ref[group, :DH] = ref[:, KEY_COLS]
    keys_ref[:, DH:] = bias_ref[:PAST, :]


GROUPS = (slice(0, CHIP_ROWS), slice(CHIP_ROWS, PAST))


def score_kernel(q_ref, partner_q_ref, keys_ref, own_top_ref, own_sum_ref, dot_ref,
                 e_ref, tops_ref, stats_ref):
    stats_ref[4:5, :] = dot_ref[...]
    for side, ref in enumerate((q_ref, partner_q_ref)):
        e_ref[:, side * COLS : (side + 1) * COLS] = dot_nt(keys_ref[...], query_tile(ref[...], side))
    for at in range(0, 2 * COLS, DH):
        side, start = divmod(at, COLS)
        cols, rows = slice(at, at + DH), slice(start, start + DH)
        tops, sums = [], []
        for i, group in enumerate(GROUPS):
            e_ref[group, cols], top, total = scored(e_ref[group, cols])
            tops_ref[i : i + 1, cols] = top
            tops.append(top)
            sums.append(total)
        if side == 0:
            tops.append(own_top_ref[:, rows])
            sums.append(own_sum_ref[:, rows])
        most = functools.reduce(jnp.maximum, tops)
        stats_ref[2 * side : 2 * side + 1, rows] = most
        stats_ref[2 * side + 1 : 2 * side + 2, rows] = sum(
            x * jnp.exp2((top - most) * EXP2_SCALING) for x, top in zip(sums, tops)
        )


def slope_kernel(g_ref, partner_g_ref, a_ref, b_ref, u_ref):
    values = jnp.concatenate([a_ref[:, VALUE_COLS], b_ref[:, VALUE_COLS]], axis=0)
    for cols, side, rows in tiles():
        u_ref[:, cols] = dot_nt(values, (g_ref, partner_g_ref)[side][rows, :])


def dot_sides(left_ref, own_ref, partner_ref):
    return dot_nn(left_ref[:, :COLS], own_ref[...]) + dot_nn(left_ref[:, COLS:], partner_ref[...])


def weigh(e_ref, u_ref, factors, row_dots, side, group, ds_ref, p_ref):
    for start in range(0, COLS, TILE):
        cols = slice(side * COLS + start, side * COLS + start + TILE)
        weights = e_ref[group, cols] * factors[:, start : start + TILE]
        slopes = u_ref[group, cols] - row_dots[:, start : start + TILE]
        ds_ref[:, cols] = (weights * slopes).astype(jnp.bfloat16)
        p_ref[:, cols] = weights.astype(jnp.bfloat16)


def key_sums(q_ref, partner_q_ref, g_ref, partner_g_ref, ds_ref, p_ref, part_ref):
    part_ref[:, KEY_COLS] = (dot_sides(ds_ref, q_ref, partner_q_ref) * SCALING).astype(jnp.bfloat16)
    part_ref[:, VALUE_COLS] = dot_sides(p_ref, g_ref, partner_g_ref).astype(jnp.bfloat16)


def main_kernel(q_ref, partner_q_ref, g_ref, partner_g_ref, e_ref, u_ref, tops_ref, stats_ref, far_ref,
                part_ref, ds_ref, norm_ref, factors_ref, p_ref):
    for side in range(2):
        near, far = 2 * side, 2 - 2 * side
        top, far_top = stats_ref[near : near + 1, :], far_ref[far : far + 1, :]
        most = jnp.maximum(top, far_top)
        total = stats_ref[near + 1 : near + 2, :] * jnp.exp2(
            (top - most) * EXP2_SCALING
        ) + far_ref[far + 1 : far + 2, :] * jnp.exp2((far_top - most) * EXP2_SCALING)
        columns = slice(side * COLS, (side + 1) * COLS)
        norm_ref[0:1, columns] = most
        norm_ref[1:2, columns] = total
        factors = jnp.exp2((tops_ref[:, columns] - most) * EXP2_SCALING) * (1.0 / total)
        row_dots = (stats_ref, far_ref)[side][4:5, :]
        factors_ref[0:1, columns] = factors[0:1]
        factors_ref[1:2, columns] = row_dots
        weigh(e_ref, u_ref, factors[1:2], row_dots, side, GROUPS[1], ds_ref, p_ref)
    key_sums(q_ref, partner_q_ref, g_ref, partner_g_ref, ds_ref, p_ref, part_ref)


def rest_kernel(q_ref, partner_q_ref, g_ref, partner_g_ref, e_ref, u_ref, factors_ref,
                part_ref, ds_ref, p_ref):
    for side in range(2):
        factors = factors_ref[:, side * COLS : (side + 1) * COLS]
        weigh(e_ref, u_ref, factors[0:1], factors[1:2], side, GROUPS[0], ds_ref, p_ref)
    key_sums(q_ref, partner_q_ref, g_ref, partner_g_ref, ds_ref, p_ref, part_ref)


def total_kernel(back_ref, own_ref, total_ref):
    total_ref[...] = back_ref[...].astype(jnp.float32) + own_ref[...]


def finish_kernel(q_ref, g_ref, dot_ref, own_e_ref, own_top_ref, norm_ref, near_ds_ref, ds_ref, own_ref, a_ref, b_ref,
                  dq_ref, own_sum_ref, *rest):
    *piece_refs, own_p_ref, own_ds_ref = rest
    past_keys = jnp.concatenate([a_ref[:, KEY_COLS], b_ref[:, KEY_COLS]], axis=0)
    for cols, side, rows in reversed(list(tiles())):
        ds = jnp.concatenate([near_ds_ref[:, cols], ds_ref[:, cols]], axis=0)
        grads = dot_tn(past_keys, ds)
        if side == 0:
            slopes = dot_nt(own_ref[:, VALUE_COLS], g_ref[rows, :]) - dot_ref[:, rows]
            factor = jnp.exp2((own_top_ref[:, rows] - norm_ref[0:1, rows]) * EXP2_SCALING)
            weights = own_e_ref[:, rows] * (factor / norm_ref[1:2, rows])
            own_ds = (weights * slopes).astype(jnp.bfloat16)
            own_p_ref[:, rows] = weights.astype(jnp.bfloat16)
            own_ds_ref[:, rows] = own_ds
            grads = grads + dot_tn(own_ref[:, KEY_COLS], own_ds)
        grads = grads * SCALING
        for j in range(TILE // DH):
            pair = grads[:, j * DH : (j + 1) * DH].T
            at = rows.start + j * DH
            if side == 0:
                dq_ref[at : at + DH, :] = pair
                continue
            for start, ref in zip(PIECES, piece_refs):
                low, high = max(at, start), min(at + DH, start + ref.shape[0])
                if low < high:
                    ref[low - start : high - start, :] = pair[low - at : high - at].astype(jnp.bfloat16)
    own_sum_ref[:, KEY_COLS] = dot_nn(own_ds_ref[...], q_ref[...]) * SCALING
    own_sum_ref[:, VALUE_COLS] = dot_nn(own_p_ref[...], g_ref[...])


def add_kernel(dq_ref, *refs):
    *piece_refs, sum_ref = refs
    for h in range(HQ):
        total = dq_ref[h * ROWS : (h + 1) * ROWS, :]
        low = h * ROWS
        parts = []
        for start, ref in zip(PIECES, piece_refs):
            first, last = max(low, start), min(low + ROWS, start + ref.shape[0])
            if first < last:
                parts.append(ref[first - start : last - start, :].astype(jnp.float32))
        partner = parts[0] if len(parts) == 1 else jnp.concatenate(parts, axis=0)
        sum_ref[:, h * DH : (h + 1) * DH] = (total + partner).astype(jnp.bfloat16)


def call(kernel, outs, scratch=(), flops=10**9):
    vmem = pl.BlockSpec(memory_space=pltpu.VMEM)
    return lambda *args: pl.pallas_call(
        kernel,
        out_shape=outs,
        in_specs=[vmem] * len(args),
        out_specs=[vmem] * len(outs),
        scratch_shapes=list(scratch),
        compiler_params=pltpu.CompilerParams(vmem_limit_bytes=24 * 1024 * 1024),
        cost_estimate=pl.CostEstimate(flops=flops, bytes_accessed=flops // 500, transcendentals=0),
    )(*args)


def on_device(query_rows, key_rows, value_rows, saved_out, out_grad, doc_lengths):
    shape = jax.ShapeDtypeStruct
    bf16, f32 = jnp.bfloat16, jnp.float32
    together = lax.optimization_barrier
    other = (swap_cores(key_rows), swap_cores(value_rows))
    mine = jnp.concatenate([key_rows, value_rows], axis=1)
    other, mine = together((other, mine))
    own = call(pack_kernel, [shape((CHIP_ROWS, 2 * DH), bf16)])(mine, *other)[0]
    fetched = [move_chips(own, number, True) for number in range(2)]
    columns = 2 * COLS
    q2 = call(layout_kernel, [shape((COLS, DH), bf16)], flops=10**8)(query_rows)[0]
    g2, row_dot, bias, own_weights, own_top, own_sum = call(
        prepare_kernel,
        [shape((COLS, DH), bf16), shape((1, COLS), f32),
         shape((PAST + CHIP_ROWS, DH), bf16), shape((CHIP_ROWS, COLS), f32), shape((1, COLS), f32),
         shape((1, COLS), f32)],
        flops=10**8,
    )(q2, saved_out, out_grad, doc_lengths.reshape(1, 64), own)
    keys = call(keys_kernel, [shape((PAST, 2 * DH), bf16)], flops=4 * 10**9)(*fetched, bias)[0]
    q3, g3 = swap_cores(q2), swap_cores(g2)
    weights, tops, stats = call(
        score_kernel, [shape((PAST, columns), f32), shape((2, columns), f32), shape((5, COLS), f32)]
    )(q2, q3, keys, own_top, own_sum, row_dot)
    far_stats = swap_cores(stats)
    slopes = call(slope_kernel, [shape((PAST, columns), f32)])(g2, g3, *fetched)[0]
    far_stats, slopes = together((far_stats, slopes))
    part_b, ds, norm, factors = call(
        main_kernel,
        [shape((CHIP_ROWS, 2 * DH), bf16), shape((CHIP_ROWS, columns), bf16), shape((2, columns), f32),
         shape((2, columns), f32)],
        [pltpu.VMEM((CHIP_ROWS, columns), bf16)],
    )(q2, q3, g2, g3, weights, slopes, tops, stats, far_stats)
    part_a, near_ds = call(
        rest_kernel,
        [shape((CHIP_ROWS, 2 * DH), bf16), shape((CHIP_ROWS, columns), bf16)],
        [pltpu.VMEM((CHIP_ROWS, columns), bf16)],
    )(q2, q3, g2, g3, weights, slopes, factors)
    back = [move_chips(part, number, False) for number, part in enumerate((part_a, part_b))]
    query_grad, own_sums, *pieces = call(
        finish_kernel,
        [shape((COLS, DH), f32), shape((CHIP_ROWS, 2 * DH), f32)]
        + [shape((high - low, DH), bf16) for low, high in zip(PIECES, PIECES[1:])],
        [pltpu.VMEM((CHIP_ROWS, COLS), bf16)] * 2,
        flops=10**8,
    )(q2, g2, row_dot, own_weights, own_top, norm, near_ds, ds, own, *fetched)
    pieces = [swap_cores(piece) for piece in pieces]
    totals = call(total_kernel, [shape((CHIP_ROWS, 2 * DH), f32)], flops=5 * 10**9)(back[1], own_sums)[0]
    totals = totals + back[0].astype(f32)
    far_totals = swap_cores(totals[ROWS:].astype(bf16))
    totals, query_grad = together((totals, query_grad))
    query_grad = call(add_kernel, [shape((ROWS, HQ * DH), bf16)])(query_grad, *pieces)[0]
    far_totals, query_grad = together((far_totals, query_grad))
    result = totals[:ROWS] + far_totals.astype(f32)
    result = result.astype(bf16)
    return (query_grad, result[:, :DH], result[:, DH:])


def solution(mesh):
    placed = P(AXES, None)
    return jax.shard_map(
        on_device,
        mesh=mesh,
        in_specs=(placed,) * 5 + (P(),),
        out_specs=(placed,) * 3,
        check_vma=False,
    )
```

```python
import functools
import math

import jax
import jax.numpy as jnp
from jax import lax
from jax.experimental import pallas as pl
from jax.experimental.pallas import tpu as pltpu
from jax.sharding import PartitionSpec as P

DH = 128
HQ = 16
ROWS = 64
CHUNKS = 256
CHIPS = CHUNKS // 2
HALF_CHUNKS = 8
HALVES = CHUNKS // HALF_CHUNKS
COLS = HQ * ROWS
CHIP_ROWS = 2 * ROWS
PAST = 2 * CHIP_ROWS
TILE = 1024
TILES = COLS // TILE
NEG = -1e30
SCALING = 1.0 / math.sqrt(DH)
EXP2_SCALING = SCALING * math.log2(math.e)
AXES = ("blk", "uly")
MOVES = (
    ((1, 4), (0, 0, 0, 1), (1, 0, 0, 0)),
    ((3, 2), (0, 1, 0, 0), (0, 0, 1, 0)),
)
PIECES = (0, 512, COLS)
KEY_COLS, VALUE_COLS = slice(0, DH), slice(DH, 2 * DH)


def device_of(chunk):
    half, place = divmod(chunk, HALF_CHUNKS)
    if half < HALVES // 2:
        return half * 16 + place
    return (HALVES - 1 - half) * 16 + 8 + place


def swap_cores(x):
    return lax.ppermute(x, "uly", [(i, i ^ 1) for i in range(16)])


def move_chips(x, number, forward):
    steps, sends, takes = MOVES[number]
    pairs = []
    for chip in range(CHIPS):
        for other, step in enumerate(steps):
            target = (chip + step) % CHIPS
            source = 2 * chip + (sends[chip % 4] ^ other)
            pair = (device_of(source), device_of(2 * target + (takes[target % 4] ^ other)))
            pairs.append(pair if forward else pair[::-1])
    return lax.ppermute(x, AXES, pairs)


def entry(table, index):
    value = table[3]
    for i in range(3):
        value = jnp.where(index == i, table[i], value)
    return value


def dot(a, b, contract):
    return lax.dot_general(a, b, (contract, ((), ())), preferred_element_type=jnp.float32)


def dot_nt(a, b):
    return dot(a, b, ((1,), (1,)))


def dot_nn(a, b):
    return dot(a, b, ((1,), (0,)))


def dot_tn(a, b):
    return dot(a, b, ((0,), (0,)))


def pack_kernel(mine_ref, other_k_ref, other_v_ref, w_ref):
    w_ref[:ROWS, :] = mine_ref[...]
    w_ref[ROWS:, :DH] = other_k_ref[...]
    w_ref[ROWS:, DH:] = other_v_ref[...]


def folded(x, op):
    return op(x.reshape(x.shape[0] // 8, 8, x.shape[1]), axis=0)


def tiles():
    for tile in range(2 * TILES):
        side, at = divmod(tile, TILES)
        yield slice(tile * TILE, (tile + 1) * TILE), side, slice(at * TILE, (at + 1) * TILE)


def query_tile(queries, side):
    row = lax.rem(lax.broadcasted_iota(jnp.int32, (DH, DH), 0), ROWS) + side * ROWS
    lane = lax.broadcasted_iota(jnp.int32, (DH, DH), 1)
    hot = (row == lane).astype(jnp.bfloat16)
    return jnp.concatenate([queries, jnp.concatenate([hot] * (queries.shape[0] // DH), axis=0)], axis=1)


def scored(scores):
    top = jnp.max(folded(scores, jnp.max), axis=0, keepdims=True)
    weights = jnp.exp2((scores - top) * EXP2_SCALING)
    return weights, top, jnp.sum(folded(weights, jnp.sum), axis=0, keepdims=True)


def layout_kernel(q_ref, q2_ref):
    for h in range(HQ):
        q2_ref[h * ROWS : (h + 1) * ROWS, :] = q_ref[:, h * DH : (h + 1) * DH]


def prepare_kernel(q2_ref, o_ref, g_ref, len_ref, own_ref,
                   g2_ref, dot_ref, bias_ref, e_ref, top_ref, sum_ref):
    blk = lax.axis_index("blk")
    uly = lax.axis_index("uly")
    core = lax.rem(uly, 2)
    place = lax.rem(uly, HALF_CHUNKS)
    half = jnp.where(uly < HALF_CHUNKS, blk, HALVES - 1 - blk)
    chunk = half * HALF_CHUNKS + place
    chip = chunk // 2

    ones = jnp.ones((8, DH), jnp.bfloat16)
    for h in range(HQ):
        cols = slice(h * DH, (h + 1) * DH)
        rows = slice(h * ROWS, (h + 1) * ROWS)
        grad = g_ref[:, cols]
        g2_ref[rows, :] = grad
        prod = grad.astype(jnp.float32) * o_ref[:, cols].astype(jnp.float32)
        high = prod.astype(jnp.bfloat16)
        low = (prod - high.astype(jnp.float32)).astype(jnp.bfloat16)
        dot_ref[:, rows] = (dot_nt(ones, high) + dot_nt(ones, low))[0:1]

    lens = jnp.broadcast_to(len_ref[...].astype(jnp.float32), (64, 64))
    doc = lax.broadcasted_iota(jnp.int32, (64, 64), 0)
    other = lax.broadcasted_iota(jnp.int32, (64, 64), 1)
    starts = jnp.sum(jnp.where(other < doc, lens, 0.0), axis=1, keepdims=True).astype(jnp.int32)
    lane = lax.broadcasted_iota(jnp.int32, (1, DH), 1)
    here = jnp.where(lane < ROWS, chunk, 2 * chip + 1 - core) * ROWS + lax.rem(lane, ROWS)
    first = jnp.max(jnp.where(starts <= here, starts, 0), axis=0, keepdims=True)
    index = lax.broadcasted_iota(jnp.int32, (ROWS, DH), 0)
    chunks = []
    place = lax.rem(chip, 4)
    for (first_step, second_step), sends, takes in MOVES:
        is_first = core == entry(takes, place)
        source = jnp.where(
            is_first,
            entry([sends[(y - first_step) % 4] for y in range(4)], place),
            entry([1 - sends[(y - second_step) % 4] for y in range(4)], place),
        )
        past = 2 * (chip - jnp.where(is_first, first_step, second_step))
        chunks += [past + source, past + 1 - source]
    for part, key_chunk in enumerate(chunks + [chunk, 2 * chip + 1 - core]):
        where = key_chunk * ROWS + index
        bias = jnp.where((where >= first) & (where <= here), 0.0, NEG).astype(jnp.bfloat16)
        bias_ref[part * ROWS : (part + 1) * ROWS, :] = bias
    keys = jnp.concatenate([own_ref[:, KEY_COLS], bias_ref[PAST:, :]], axis=1)
    for tile in range(TILES):
        cols = slice(tile * TILE, (tile + 1) * TILE)
        e_ref[:, cols], top_ref[:, cols], sum_ref[:, cols] = scored(
            dot_nt(keys, query_tile(q2_ref[cols, :], 0))
        )


def keys_kernel(a_ref, b_ref, bias_ref, keys_ref):
    for ref, group in zip((a_ref, b_ref), GROUPS):
        keys_ref[group, :DH] = ref[:, KEY_COLS]
    keys_ref[:, DH:] = bias_ref[:PAST, :]


GROUPS = (slice(0, CHIP_ROWS), slice(CHIP_ROWS, PAST))


def score_kernel(q_ref, partner_q_ref, keys_ref, own_top_ref, own_sum_ref, dot_ref,
                 e_ref, tops_ref, stats_ref):
    stats_ref[4:5, :] = dot_ref[...]
    for side, ref in enumerate((q_ref, partner_q_ref)):
        e_ref[:, side * COLS : (side + 1) * COLS] = dot_nt(keys_ref[...], query_tile(ref[...], side))
    for at in range(0, 2 * COLS, DH):
        side, start = divmod(at, COLS)
        cols, rows = slice(at, at + DH), slice(start, start + DH)
        tops, sums = [], []
        for i, group in enumerate(GROUPS):
            e_ref[group, cols], top, total = scored(e_ref[group, cols])
            tops_ref[i : i + 1, cols] = top
            tops.append(top)
            sums.append(total)
        if side == 0:
            tops.append(own_top_ref[:, rows])
            sums.append(own_sum_ref[:, rows])
        most = functools.reduce(jnp.maximum, tops)
        stats_ref[2 * side : 2 * side + 1, rows] = most
        stats_ref[2 * side + 1 : 2 * side + 2, rows] = sum(
            x * jnp.exp2((top - most) * EXP2_SCALING) for x, top in zip(sums, tops)
        )


def slope_kernel(g_ref, partner_g_ref, a_ref, b_ref, u_ref):
    values = jnp.concatenate([a_ref[:, VALUE_COLS], b_ref[:, VALUE_COLS]], axis=0)
    for cols, side, rows in tiles():
        u_ref[:, cols] = dot_nt(values, (g_ref, partner_g_ref)[side][rows, :])


def dot_sides(left_ref, own_ref, partner_ref):
    return dot_nn(left_ref[:, :COLS], own_ref[...]) + dot_nn(left_ref[:, COLS:], partner_ref[...])


def weigh(e_ref, u_ref, factors, row_dots, side, group, ds_ref, p_ref):
    for start in range(0, COLS, TILE):
        cols = slice(side * COLS + start, side * COLS + start + TILE)
        weights = e_ref[group, cols] * factors[:, start : start + TILE]
        slopes = u_ref[group, cols] - row_dots[:, start : start + TILE]
        ds_ref[:, cols] = (weights * slopes).astype(jnp.bfloat16)
        p_ref[:, cols] = weights.astype(jnp.bfloat16)


def key_sums(q_ref, partner_q_ref, g_ref, partner_g_ref, ds_ref, p_ref, part_ref):
    part_ref[:, KEY_COLS] = (dot_sides(ds_ref, q_ref, partner_q_ref) * SCALING).astype(jnp.bfloat16)
    part_ref[:, VALUE_COLS] = dot_sides(p_ref, g_ref, partner_g_ref).astype(jnp.bfloat16)


def main_kernel(q_ref, partner_q_ref, g_ref, partner_g_ref, e_ref, u_ref, tops_ref, stats_ref, far_ref,
                part_ref, ds_ref, norm_ref, factors_ref, p_ref):
    for side in range(2):
        near, far = 2 * side, 2 - 2 * side
        top, far_top = stats_ref[near : near + 1, :], far_ref[far : far + 1, :]
        most = jnp.maximum(top, far_top)
        total = stats_ref[near + 1 : near + 2, :] * jnp.exp2(
            (top - most) * EXP2_SCALING
        ) + far_ref[far + 1 : far + 2, :] * jnp.exp2((far_top - most) * EXP2_SCALING)
        columns = slice(side * COLS, (side + 1) * COLS)
        norm_ref[0:1, columns] = most
        norm_ref[1:2, columns] = total
        factors = jnp.exp2((tops_ref[:, columns] - most) * EXP2_SCALING) * (1.0 / total)
        row_dots = (stats_ref, far_ref)[side][4:5, :]
        factors_ref[0:1, columns] = factors[0:1]
        factors_ref[1:2, columns] = row_dots
        weigh(e_ref, u_ref, factors[1:2], row_dots, side, GROUPS[1], ds_ref, p_ref)
    key_sums(q_ref, partner_q_ref, g_ref, partner_g_ref, ds_ref, p_ref, part_ref)


def rest_kernel(q_ref, partner_q_ref, g_ref, partner_g_ref, e_ref, u_ref, factors_ref,
                part_ref, ds_ref, p_ref):
    for side in range(2):
        factors = factors_ref[:, side * COLS : (side + 1) * COLS]
        weigh(e_ref, u_ref, factors[0:1], factors[1:2], side, GROUPS[0], ds_ref, p_ref)
    key_sums(q_ref, partner_q_ref, g_ref, partner_g_ref, ds_ref, p_ref, part_ref)


def total_kernel(back_ref, own_ref, total_ref):
    total_ref[...] = back_ref[...].astype(jnp.float32) + own_ref[...]


def finish_kernel(q_ref, g_ref, dot_ref, own_e_ref, own_top_ref, norm_ref, near_ds_ref, ds_ref, own_ref, a_ref, b_ref,
                  dq_ref, own_sum_ref, *rest):
    *piece_refs, own_p_ref, own_ds_ref = rest
    past_keys = jnp.concatenate([a_ref[:, KEY_COLS], b_ref[:, KEY_COLS]], axis=0)
    for cols, side, rows in reversed(list(tiles())):
        ds = jnp.concatenate([near_ds_ref[:, cols], ds_ref[:, cols]], axis=0)
        grads = dot_tn(past_keys, ds)
        if side == 0:
            slopes = dot_nt(own_ref[:, VALUE_COLS], g_ref[rows, :]) - dot_ref[:, rows]
            factor = jnp.exp2((own_top_ref[:, rows] - norm_ref[0:1, rows]) * EXP2_SCALING)
            weights = own_e_ref[:, rows] * (factor / norm_ref[1:2, rows])
            own_ds = (weights * slopes).astype(jnp.bfloat16)
            own_p_ref[:, rows] = weights.astype(jnp.bfloat16)
            own_ds_ref[:, rows] = own_ds
            grads = grads + dot_tn(own_ref[:, KEY_COLS], own_ds)
        grads = grads * SCALING
        for j in range(TILE // DH):
            pair = grads[:, j * DH : (j + 1) * DH].T
            at = rows.start + j * DH
            if side == 0:
                dq_ref[at : at + DH, :] = pair
                continue
            for start, ref in zip(PIECES, piece_refs):
                low, high = max(at, start), min(at + DH, start + ref.shape[0])
                if low < high:
                    ref[low - start : high - start, :] = pair[low - at : high - at].astype(jnp.bfloat16)
    own_sum_ref[:, KEY_COLS] = dot_nn(own_ds_ref[...], q_ref[...]) * SCALING
    own_sum_ref[:, VALUE_COLS] = dot_nn(own_p_ref[...], g_ref[...])


def add_kernel(dq_ref, *refs):
    *piece_refs, sum_ref = refs
    for h in range(HQ):
        total = dq_ref[h * ROWS : (h + 1) * ROWS, :]
        low = h * ROWS
        parts = []
        for start, ref in zip(PIECES, piece_refs):
            first, last = max(low, start), min(low + ROWS, start + ref.shape[0])
            if first < last:
                parts.append(ref[first - start : last - start, :].astype(jnp.float32))
        partner = parts[0] if len(parts) == 1 else jnp.concatenate(parts, axis=0)
        sum_ref[:, h * DH : (h + 1) * DH] = (total + partner).astype(jnp.bfloat16)


def call(kernel, outs, scratch=(), flops=10**9):
    vmem = pl.BlockSpec(memory_space=pltpu.VMEM)
    return lambda *args: pl.pallas_call(
        kernel,
        out_shape=outs,
        in_specs=[vmem] * len(args),
        out_specs=[vmem] * len(outs),
        scratch_shapes=list(scratch),
        compiler_params=pltpu.CompilerParams(vmem_limit_bytes=24 * 1024 * 1024),
        cost_estimate=pl.CostEstimate(flops=flops, bytes_accessed=flops // 500, transcendentals=0),
    )(*args)


def on_device(query_rows, key_rows, value_rows, saved_out, out_grad, doc_lengths):
    shape = jax.ShapeDtypeStruct
    bf16, f32 = jnp.bfloat16, jnp.float32
    together = lax.optimization_barrier
    other = (swap_cores(key_rows), swap_cores(value_rows))
    mine = jnp.concatenate([key_rows, value_rows], axis=1)
    other, mine = together((other, mine))
    own = call(pack_kernel, [shape((CHIP_ROWS, 2 * DH), bf16)])(mine, *other)[0]
    fetched = [move_chips(own, number, True) for number in range(2)]
    columns = 2 * COLS
    q2 = call(layout_kernel, [shape((COLS, DH), bf16)], flops=10**8)(query_rows)[0]
    g2, row_dot, bias, own_weights, own_top, own_sum = call(
        prepare_kernel,
        [shape((COLS, DH), bf16), shape((1, COLS), f32),
         shape((PAST + CHIP_ROWS, DH), bf16), shape((CHIP_ROWS, COLS), f32), shape((1, COLS), f32),
         shape((1, COLS), f32)],
        flops=10**8,
    )(q2, saved_out, out_grad, doc_lengths.reshape(1, 64), own)
    keys = call(keys_kernel, [shape((PAST, 2 * DH), bf16)], flops=4 * 10**9)(*fetched, bias)[0]
    q3, g3 = swap_cores(q2), swap_cores(g2)
    weights, tops, stats = call(
        score_kernel, [shape((PAST, columns), f32), shape((2, columns), f32), shape((5, COLS), f32)]
    )(q2, q3, keys, own_top, own_sum, row_dot)
    far_stats = swap_cores(stats)
    slopes = call(slope_kernel, [shape((PAST, columns), f32)])(g2, g3, *fetched)[0]
    far_stats, slopes = together((far_stats, slopes))
    part_b, ds, norm, factors = call(
        main_kernel,
        [shape((CHIP_ROWS, 2 * DH), bf16), shape((CHIP_ROWS, columns), bf16), shape((2, columns), f32),
         shape((2, columns), f32)],
        [pltpu.VMEM((CHIP_ROWS, columns), bf16)],
    )(q2, q3, g2, g3, weights, slopes, tops, stats, far_stats)
    part_a, near_ds = call(
        rest_kernel,
        [shape((CHIP_ROWS, 2 * DH), bf16), shape((CHIP_ROWS, columns), bf16)],
        [pltpu.VMEM((CHIP_ROWS, columns), bf16)],
    )(q2, q3, g2, g3, weights, slopes, factors)
    back = [move_chips(part, number, False) for number, part in enumerate((part_a, part_b))]
    query_grad, own_sums, *pieces = call(
        finish_kernel,
        [shape((COLS, DH), f32), shape((CHIP_ROWS, 2 * DH), f32)]
        + [shape((high - low, DH), bf16) for low, high in zip(PIECES, PIECES[1:])],
        [pltpu.VMEM((CHIP_ROWS, COLS), bf16)] * 2,
        flops=10**8,
    )(q2, g2, row_dot, own_weights, own_top, norm, near_ds, ds, own, *fetched)
    pieces = [swap_cores(piece) for piece in pieces]
    totals = call(total_kernel, [shape((CHIP_ROWS, 2 * DH), f32)], flops=5 * 10**9)(back[1], own_sums)[0]
    totals = totals + back[0].astype(f32)
    far_totals = swap_cores(totals[ROWS:].astype(bf16))
    totals, query_grad = together((totals, query_grad))
    query_grad = call(add_kernel, [shape((ROWS, HQ * DH), bf16)])(query_grad, *pieces)[0]
    far_totals, query_grad = together((far_totals, query_grad))
    result = totals[:ROWS] + far_totals.astype(f32)
    result = result.astype(bf16)
    return (query_grad, result[:, :DH], result[:, DH:])


def solution(mesh):
    placed = P(AXES, None)
    return jax.shard_map(
        on_device,
        mesh=mesh,
        in_specs=(placed,) * 5 + (P(),),
        out_specs=(placed,) * 3,
        check_vma=False,
    )
```

```python
import functools
import math

import jax
import jax.numpy as jnp
from jax import lax
from jax.experimental import pallas as pl
from jax.experimental.pallas import tpu as pltpu
from jax.sharding import PartitionSpec as P

DH = 128
HQ = 16
ROWS = 64
CHUNKS = 256
CHIPS = CHUNKS // 2
HALF_CHUNKS = 8
HALVES = CHUNKS // HALF_CHUNKS
COLS = HQ * ROWS
CHIP_ROWS = 2 * ROWS
PAST = 2 * CHIP_ROWS
TILE = 1024
TILES = COLS // TILE
NEG = -1e30
SCALING = 1.0 / math.sqrt(DH)
EXP2_SCALING = SCALING * math.log2(math.e)
AXES = ("blk", "uly")
MOVES = (
    ((1, 4), (0, 0, 0, 1), (1, 0, 0, 0)),
    ((3, 2), (0, 0, 0, 0), (1, 1, 1, 1)),
)
PIECES = (0, 352, 704, COLS)
KEY_COLS, VALUE_COLS = slice(0, DH), slice(DH, 2 * DH)


def device_of(chunk):
    half, place = divmod(chunk, HALF_CHUNKS)
    if half < HALVES // 2:
        return half * 16 + place
    return (HALVES - 1 - half) * 16 + 8 + place


def swap_cores(x):
    return lax.ppermute(x, "uly", [(i, i ^ 1) for i in range(16)])


def move_chips(x, number, forward):
    steps, sends, takes = MOVES[number]
    pairs = []
    for chip in range(CHIPS):
        for other, step in enumerate(steps):
            target = (chip + step) % CHIPS
            source = 2 * chip + (sends[chip % 4] ^ other)
            pair = (device_of(source), device_of(2 * target + (takes[target % 4] ^ other)))
            pairs.append(pair if forward else pair[::-1])
    return lax.ppermute(x, AXES, pairs)


def entry(table, index):
    value = table[3]
    for i in range(3):
        value = jnp.where(index == i, table[i], value)
    return value


def dot(a, b, contract):
    return lax.dot_general(a, b, (contract, ((), ())), preferred_element_type=jnp.float32)


def dot_nt(a, b):
    return dot(a, b, ((1,), (1,)))


def dot_nn(a, b):
    return dot(a, b, ((1,), (0,)))


def dot_tn(a, b):
    return dot(a, b, ((0,), (0,)))


def pack_kernel(mine_ref, other_k_ref, other_v_ref, w_ref):
    w_ref[:ROWS, :] = mine_ref[...]
    w_ref[ROWS:, :DH] = other_k_ref[...]
    w_ref[ROWS:, DH:] = other_v_ref[...]


def folded(x, op):
    return op(x.reshape(x.shape[0] // 8, 8, x.shape[1]), axis=0)


def tiles():
    for tile in range(2 * TILES):
        side, at = divmod(tile, TILES)
        yield slice(tile * TILE, (tile + 1) * TILE), side, slice(at * TILE, (at + 1) * TILE)


def query_tile(queries, side):
    row = lax.rem(lax.broadcasted_iota(jnp.int32, (DH, DH), 0), ROWS) + side * ROWS
    lane = lax.broadcasted_iota(jnp.int32, (DH, DH), 1)
    hot = (row == lane).astype(jnp.bfloat16)
    return jnp.concatenate([queries, jnp.concatenate([hot] * (queries.shape[0] // DH), axis=0)], axis=1)


def scored(scores):
    top = jnp.max(folded(scores, jnp.max), axis=0, keepdims=True)
    weights = jnp.exp2((scores - top) * EXP2_SCALING)
    return weights, top, jnp.sum(folded(weights, jnp.sum), axis=0, keepdims=True)


def layout_kernel(q_ref, q2_ref):
    for h in range(HQ):
        q2_ref[h * ROWS : (h + 1) * ROWS, :] = q_ref[:, h * DH : (h + 1) * DH]


def prepare_kernel(q2_ref, o_ref, g_ref, len_ref, own_ref,
                   g2_ref, dot_ref, bias_ref, e_ref, top_ref, sum_ref):
    blk = lax.axis_index("blk")
    uly = lax.axis_index("uly")
    core = lax.rem(uly, 2)
    place = lax.rem(uly, HALF_CHUNKS)
    half = jnp.where(uly < HALF_CHUNKS, blk, HALVES - 1 - blk)
    chunk = half * HALF_CHUNKS + place
    chip = chunk // 2

    ones = jnp.ones((8, DH), jnp.bfloat16)
    for h in range(HQ):
        cols = slice(h * DH, (h + 1) * DH)
        rows = slice(h * ROWS, (h + 1) * ROWS)
        grad = g_ref[:, cols]
        g2_ref[rows, :] = grad
        prod = grad.astype(jnp.float32) * o_ref[:, cols].astype(jnp.float32)
        high = prod.astype(jnp.bfloat16)
        low = (prod - high.astype(jnp.float32)).astype(jnp.bfloat16)
        dot_ref[:, rows] = (dot_nt(ones, high) + dot_nt(ones, low))[0:1]

    lens = jnp.broadcast_to(len_ref[...].astype(jnp.float32), (64, 64))
    doc = lax.broadcasted_iota(jnp.int32, (64, 64), 0)
    other = lax.broadcasted_iota(jnp.int32, (64, 64), 1)
    starts = jnp.sum(jnp.where(other < doc, lens, 0.0), axis=1, keepdims=True).astype(jnp.int32)
    lane = lax.broadcasted_iota(jnp.int32, (1, DH), 1)
    here = jnp.where(lane < ROWS, chunk, 2 * chip + 1 - core) * ROWS + lax.rem(lane, ROWS)
    first = jnp.max(jnp.where(starts <= here, starts, 0), axis=0, keepdims=True)
    index = lax.broadcasted_iota(jnp.int32, (ROWS, DH), 0)
    chunks = []
    place = lax.rem(chip, 4)
    for (first_step, second_step), sends, takes in MOVES:
        is_first = core == entry(takes, place)
        source = jnp.where(
            is_first,
            entry([sends[(y - first_step) % 4] for y in range(4)], place),
            entry([1 - sends[(y - second_step) % 4] for y in range(4)], place),
        )
        past = 2 * (chip - jnp.where(is_first, first_step, second_step))
        chunks += [past + source, past + 1 - source]
    for part, key_chunk in enumerate(chunks + [chunk, 2 * chip + 1 - core]):
        where = key_chunk * ROWS + index
        bias = jnp.where((where >= first) & (where <= here), 0.0, NEG).astype(jnp.bfloat16)
        bias_ref[part * ROWS : (part + 1) * ROWS, :] = bias
    keys = jnp.concatenate([own_ref[:, KEY_COLS], bias_ref[PAST:, :]], axis=1)
    for tile in range(TILES):
        cols = slice(tile * TILE, (tile + 1) * TILE)
        e_ref[:, cols], top_ref[:, cols], sum_ref[:, cols] = scored(
            dot_nt(keys, query_tile(q2_ref[cols, :], 0))
        )


def keys_kernel(a_ref, b_ref, bias_ref, keys_ref):
    for ref, group in zip((a_ref, b_ref), GROUPS):
        keys_ref[group, :DH] = ref[:, KEY_COLS]
    keys_ref[:, DH:] = bias_ref[:PAST, :]


GROUPS = (slice(0, CHIP_ROWS), slice(CHIP_ROWS, PAST))


def score_kernel(q_ref, partner_q_ref, keys_ref, own_top_ref, own_sum_ref, dot_ref,
                 e_ref, tops_ref, stats_ref):
    stats_ref[4:5, :] = dot_ref[...]
    for side, ref in enumerate((q_ref, partner_q_ref)):
        e_ref[:, side * COLS : (side + 1) * COLS] = dot_nt(keys_ref[...], query_tile(ref[...], side))
    for at in range(0, 2 * COLS, DH):
        side, start = divmod(at, COLS)
        cols, rows = slice(at, at + DH), slice(start, start + DH)
        tops, sums = [], []
        for i, group in enumerate(GROUPS):
            e_ref[group, cols], top, total = scored(e_ref[group, cols])
            tops_ref[i : i + 1, cols] = top
            tops.append(top)
            sums.append(total)
        if side == 0:
            tops.append(own_top_ref[:, rows])
            sums.append(own_sum_ref[:, rows])
        most = functools.reduce(jnp.maximum, tops)
        stats_ref[2 * side : 2 * side + 1, rows] = most
        stats_ref[2 * side + 1 : 2 * side + 2, rows] = sum(
            x * jnp.exp2((top - most) * EXP2_SCALING) for x, top in zip(sums, tops)
        )


def slope_kernel(g_ref, partner_g_ref, a_ref, b_ref, u_ref):
    values = jnp.concatenate([a_ref[:, VALUE_COLS], b_ref[:, VALUE_COLS]], axis=0)
    for cols, side, rows in tiles():
        u_ref[:, cols] = dot_nt(values, (g_ref, partner_g_ref)[side][rows, :])


def dot_sides(left_ref, own_ref, partner_ref):
    return dot_nn(left_ref[:, :COLS], own_ref[...]) + dot_nn(left_ref[:, COLS:], partner_ref[...])


def weigh(e_ref, u_ref, factors, row_dots, side, group, ds_ref, p_ref):
    for start in range(0, COLS, TILE):
        cols = slice(side * COLS + start, side * COLS + start + TILE)
        weights = e_ref[group, cols] * factors[:, start : start + TILE]
        slopes = u_ref[group, cols] - row_dots[:, start : start + TILE]
        ds_ref[:, cols] = (weights * slopes).astype(jnp.bfloat16)
        p_ref[:, cols] = weights.astype(jnp.bfloat16)


def key_sums(q_ref, partner_q_ref, g_ref, partner_g_ref, ds_ref, p_ref, part_ref):
    part_ref[:, KEY_COLS] = (dot_sides(ds_ref, q_ref, partner_q_ref) * SCALING).astype(jnp.bfloat16)
    part_ref[:, VALUE_COLS] = dot_sides(p_ref, g_ref, partner_g_ref).astype(jnp.bfloat16)


def main_kernel(q_ref, partner_q_ref, g_ref, partner_g_ref, e_ref, u_ref, tops_ref, stats_ref, far_ref,
                part_ref, ds_ref, norm_ref, factors_ref, p_ref):
    for side in range(2):
        near, far = 2 * side, 2 - 2 * side
        top, far_top = stats_ref[near : near + 1, :], far_ref[far : far + 1, :]
        most = jnp.maximum(top, far_top)
        total = stats_ref[near + 1 : near + 2, :] * jnp.exp2(
            (top - most) * EXP2_SCALING
        ) + far_ref[far + 1 : far + 2, :] * jnp.exp2((far_top - most) * EXP2_SCALING)
        columns = slice(side * COLS, (side + 1) * COLS)
        norm_ref[0:1, columns] = most
        norm_ref[1:2, columns] = total
        factors = jnp.exp2((tops_ref[:, columns] - most) * EXP2_SCALING) * (1.0 / total)
        row_dots = (stats_ref, far_ref)[side][4:5, :]
        factors_ref[0:1, columns] = factors[0:1]
        factors_ref[1:2, columns] = row_dots
        weigh(e_ref, u_ref, factors[1:2], row_dots, side, GROUPS[1], ds_ref, p_ref)
    key_sums(q_ref, partner_q_ref, g_ref, partner_g_ref, ds_ref, p_ref, part_ref)


def rest_kernel(q_ref, partner_q_ref, g_ref, partner_g_ref, e_ref, u_ref, factors_ref,
                part_ref, ds_ref, p_ref):
    for side in range(2):
        factors = factors_ref[:, side * COLS : (side + 1) * COLS]
        weigh(e_ref, u_ref, factors[0:1], factors[1:2], side, GROUPS[0], ds_ref, p_ref)
    key_sums(q_ref, partner_q_ref, g_ref, partner_g_ref, ds_ref, p_ref, part_ref)


def total_kernel(back_ref, own_ref, total_ref):
    total_ref[...] = back_ref[...].astype(jnp.float32) + own_ref[...]


def finish_kernel(q_ref, g_ref, dot_ref, own_e_ref, own_top_ref, norm_ref, near_ds_ref, ds_ref, own_ref, a_ref, b_ref,
                  dq_ref, own_sum_ref, *rest):
    *piece_refs, own_p_ref, own_ds_ref = rest
    past_keys = jnp.concatenate([a_ref[:, KEY_COLS], b_ref[:, KEY_COLS]], axis=0)
    for cols, side, rows in reversed(list(tiles())):
        ds = jnp.concatenate([near_ds_ref[:, cols], ds_ref[:, cols]], axis=0)
        grads = dot_tn(past_keys, ds)
        if side == 0:
            slopes = dot_nt(own_ref[:, VALUE_COLS], g_ref[rows, :]) - dot_ref[:, rows]
            factor = jnp.exp2((own_top_ref[:, rows] - norm_ref[0:1, rows]) * EXP2_SCALING)
            weights = own_e_ref[:, rows] * (factor / norm_ref[1:2, rows])
            own_ds = (weights * slopes).astype(jnp.bfloat16)
            own_p_ref[:, rows] = weights.astype(jnp.bfloat16)
            own_ds_ref[:, rows] = own_ds
            grads = grads + dot_tn(own_ref[:, KEY_COLS], own_ds)
        grads = grads * SCALING
        for j in range(TILE // DH):
            pair = grads[:, j * DH : (j + 1) * DH].T
            at = rows.start + j * DH
            if side == 0:
                dq_ref[at : at + DH, :] = pair
                continue
            for start, ref in zip(PIECES, piece_refs):
                low, high = max(at, start), min(at + DH, start + ref.shape[0])
                if low < high:
                    ref[low - start : high - start, :] = pair[low - at : high - at].astype(jnp.bfloat16)
    own_sum_ref[:, KEY_COLS] = dot_nn(own_ds_ref[...], q_ref[...]) * SCALING
    own_sum_ref[:, VALUE_COLS] = dot_nn(own_p_ref[...], g_ref[...])


def add_kernel(dq_ref, *refs):
    *piece_refs, sum_ref = refs
    for h in range(HQ):
        total = dq_ref[h * ROWS : (h + 1) * ROWS, :]
        low = h * ROWS
        parts = []
        for start, ref in zip(PIECES, piece_refs):
            first, last = max(low, start), min(low + ROWS, start + ref.shape[0])
            if first < last:
                parts.append(ref[first - start : last - start, :].astype(jnp.float32))
        partner = parts[0] if len(parts) == 1 else jnp.concatenate(parts, axis=0)
        sum_ref[:, h * DH : (h + 1) * DH] = (total + partner).astype(jnp.bfloat16)


def call(kernel, outs, scratch=(), flops=10**9):
    vmem = pl.BlockSpec(memory_space=pltpu.VMEM)
    return lambda *args: pl.pallas_call(
        kernel,
        out_shape=outs,
        in_specs=[vmem] * len(args),
        out_specs=[vmem] * len(outs),
        scratch_shapes=list(scratch),
        compiler_params=pltpu.CompilerParams(vmem_limit_bytes=24 * 1024 * 1024),
        cost_estimate=pl.CostEstimate(flops=flops, bytes_accessed=flops // 500, transcendentals=0),
    )(*args)


def on_device(query_rows, key_rows, value_rows, saved_out, out_grad, doc_lengths):
    shape = jax.ShapeDtypeStruct
    bf16, f32 = jnp.bfloat16, jnp.float32
    together = lax.optimization_barrier
    other = (swap_cores(key_rows), swap_cores(value_rows))
    mine = jnp.concatenate([key_rows, value_rows], axis=1)
    other, mine = together((other, mine))
    own = call(pack_kernel, [shape((CHIP_ROWS, 2 * DH), bf16)])(mine, *other)[0]
    fetched = [move_chips(own, number, True) for number in range(2)]
    columns = 2 * COLS
    q2 = call(layout_kernel, [shape((COLS, DH), bf16)], flops=10**8)(query_rows)[0]
    g2, row_dot, bias, own_weights, own_top, own_sum = call(
        prepare_kernel,
        [shape((COLS, DH), bf16), shape((1, COLS), f32),
         shape((PAST + CHIP_ROWS, DH), bf16), shape((CHIP_ROWS, COLS), f32), shape((1, COLS), f32),
         shape((1, COLS), f32)],
        flops=10**8,
    )(q2, saved_out, out_grad, doc_lengths.reshape(1, 64), own)
    keys = call(keys_kernel, [shape((PAST, 2 * DH), bf16)], flops=4 * 10**9)(*fetched, bias)[0]
    q3, g3 = swap_cores(q2), swap_cores(g2)
    weights, tops, stats = call(
        score_kernel, [shape((PAST, columns), f32), shape((2, columns), f32), shape((5, COLS), f32)]
    )(q2, q3, keys, own_top, own_sum, row_dot)
    far_stats = swap_cores(stats)
    slopes = call(slope_kernel, [shape((PAST, columns), f32)])(g2, g3, *fetched)[0]
    far_stats, slopes = together((far_stats, slopes))
    part_b, ds, norm, factors = call(
        main_kernel,
        [shape((CHIP_ROWS, 2 * DH), bf16), shape((CHIP_ROWS, columns), bf16), shape((2, columns), f32),
         shape((2, columns), f32)],
        [pltpu.VMEM((CHIP_ROWS, columns), bf16)],
    )(q2, q3, g2, g3, weights, slopes, tops, stats, far_stats)
    part_a, near_ds = call(
        rest_kernel,
        [shape((CHIP_ROWS, 2 * DH), bf16), shape((CHIP_ROWS, columns), bf16)],
        [pltpu.VMEM((CHIP_ROWS, columns), bf16)],
    )(q2, q3, g2, g3, weights, slopes, factors)
    back = [move_chips(part, number, False) for number, part in enumerate((part_a, part_b))]
    query_grad, own_sums, *pieces = call(
        finish_kernel,
        [shape((COLS, DH), f32), shape((CHIP_ROWS, 2 * DH), f32)]
        + [shape((high - low, DH), bf16) for low, high in zip(PIECES, PIECES[1:])],
        [pltpu.VMEM((CHIP_ROWS, COLS), bf16)] * 2,
        flops=10**8,
    )(q2, g2, row_dot, own_weights, own_top, norm, near_ds, ds, own, *fetched)
    pieces = [swap_cores(piece) for piece in pieces]
    totals = call(total_kernel, [shape((CHIP_ROWS, 2 * DH), f32)], flops=5 * 10**9)(back[1], own_sums)[0]
    totals = totals + back[0].astype(f32)
    far_totals = swap_cores(totals[ROWS:].astype(bf16))
    totals, query_grad = together((totals, query_grad))
    query_grad = call(add_kernel, [shape((ROWS, HQ * DH), bf16)])(query_grad, *pieces)[0]
    far_totals, query_grad = together((far_totals, query_grad))
    result = totals[:ROWS] + far_totals.astype(f32)
    result = result.astype(bf16)
    return (query_grad, result[:, :DH], result[:, DH:])


def solution(mesh):
    placed = P(AXES, None)
    return jax.shard_map(
        on_device,
        mesh=mesh,
        in_specs=(placed,) * 5 + (P(),),
        out_specs=(placed,) * 3,
        check_vma=False,
    )
```
